32 devices in a mesh: expert: 8 (over z, y), etp: 4 (over x, core).
Axes of the slice: x: 2, y: 2, z: 4, core: 2. Of those that a mesh axis runs over, the one named last changes fastest.
Arguments:
- tokens: bfloat16 [1024, 2048], P('expert'), may hold values from -6 to 6
- grad_out: bfloat16 [1024, 2048], P('expert'), may hold values from -6 to 6
- routes: int32 [1024, 8], P('expert'), may hold values from 0 to 15, all different within a row; in each aligned block of 128 rows (0 to 127, 128 to 255, ...) at most 80 rows name the same one
- probs: bfloat16 [1024, 8], P('expert'), may hold values from 0.049804688 to 0.3984375
- w_gate: bfloat16 [16, 768, 2048], P('expert', 'etp'), may hold values from -0.125 to 0.125
- w_up: bfloat16 [16, 768, 2048], P('expert', 'etp'), may hold values from -0.125 to 0.125
- w_down: bfloat16 [16, 768, 2048], P('expert', 'etp'), may hold values from -0.21875 to 0.21875
Outputs:
- grad_tokens: bfloat16 [1024, 2048], P('expert')
- grad_probs: bfloat16 [1024, 8], P('expert')
- grad_gate: bfloat16 [16, 768, 2048], P('expert', 'etp')
- grad_up: bfloat16 [16, 768, 2048], P('expert', 'etp')
- grad_down: bfloat16 [16, 768, 2048], P('expert', 'etp')
The draws below stay inside these ranges and needn't reach their ends.
Inputs may be any that keep to these rules, and one draw needn't show every extreme that they name: `routes`: each row names 8 different experts. Among the 128 rows of one device no expert is named by more than 80 rows, a bound that some block reaches.
All inputs are finite; a program needn't handle non-finite values.
Results may differ from the reference program's by a relative error of at most 0.018.
Values may be sent and summed in bfloat16 or wider, within the bound.
No kernel may reach another device: no remote copies, remote signals or barrier semaphores. Data moves between devices by JAX's collectives and lax.ppermute only.
A program may use at most 128 MiB of HBM per device.

```python
import math
import jax
import jax.numpy as jnp
import numpy as np
from jax import lax

D = 2048
FF = 768
TOP = 8
TOK_DEV = 128
EXPERTS = 16
TOKENS = 1024
MOST = 80
HID_DEV = 192
N_EXPERT = 8
N_ETP = 4


def steps_of(stream_key, dims, cuts, low, high):
    loudness, own = 1.0, jax.random.fold_in(stream_key, 6)
    for dim, shards_of in cuts:
        heights = jnp.exp(jax.random.uniform(jax.random.fold_in(own, dim), (shards_of,), jnp.float32, low / len(cuts), high / len(cuts)))
        loudness = loudness * jnp.repeat(heights, dims[dim] // shards_of).reshape([-1 if axis == dim else 1 for axis in range(len(dims))])
    return loudness


def routed_block(own_key, own, number, rows, count, top, reach, lean):
    sequence = jax.random.permutation(own_key, count)
    packed, ordinary = shares(count, rows * top, reach, lean, True), shares(count, rows * top, reach, lean, False)
    places = jnp.arange(count)

    def named(sizes, offset_by):
        used = int((sizes > 0).sum())
        fixed = max(1, used // 4)
        passed = fixed + (places - fixed + offset_by * (used - fixed)) % max(1, count - fixed)
        return jnp.zeros((count,), jnp.int32).at[sequence[jnp.where(places < fixed, places, passed)]].set(jnp.asarray(sizes, jnp.int32))

    sizes = jnp.where(number % 4 == 0, named(packed, number // 4), named(ordinary, number - number // 4 - 1))
    mixed = jax.random.permutation(jax.random.fold_in(own, 3), count)
    source_of, taker = mixed[0:count // 2 * 2:2], mixed[1:count // 2 * 2:2]
    room = jnp.minimum(sizes[source_of] - 1, reach - sizes[taker]) // 2
    room = jnp.where((source_of == sequence[0]) | (taker == sequence[0]) | (sizes[taker] == 0), 0, jnp.maximum(room, 0))
    passed = jax.random.randint(jax.random.fold_in(own, 4), (count // 2,), 0, 1 << 20) % (room + 1)
    sizes = sizes.at[source_of].add(-passed).at[taker].add(passed)
    members = jnp.searchsorted(jnp.cumsum(sizes), jnp.arange(rows * top), side="right").astype(jnp.int32)
    grid = members.reshape(top, rows).T
    grid = grid[jax.random.permutation(jax.random.fold_in(own, 1), rows)]
    offset_by = jax.random.randint(jax.random.fold_in(own, 2), (rows, 1), 0, top)
    return jnp.take_along_axis(grid, (jnp.arange(top)[None, :] + offset_by) % top, axis=1)


def shares(number_of, total, bound, slope, full):
    portions = [(1 << 20) // math.isqrt(grade ** slope) + 1 for grade in range(1, number_of + 1)]
    largest = bound if full else min(bound, max(-(-total // number_of), total * portions[0] // sum(portions)))
    least = 1 if total - largest >= number_of - 1 else 0
    given, rest = [largest] + [least] * (number_of - 1), total - largest - least * (number_of - 1)
    while rest > 0:
        movable = [i for i in range(1, number_of) if given[i] < largest] or [i for i in range(1, number_of) if given[i] < bound]
        pool, budget = sum([portions[i] for i in movable]), rest
        for i in movable:
            extra = min(bound - given[i], max(1, budget * portions[i] // pool), rest)
            given[i] = given[i] + extra
            rest = rest - extra
    return np.array(given)


def scatter_about(key, shape, width, most, split=(), kind=jnp.bfloat16):
    gain = steps_of(key, shape, split, -0.22, 0.18) if split else 1.0
    result = jax.random.normal(key, shape, jnp.float32) * width * gain
    return jnp.minimum(jnp.maximum(result, -most), most).astype(kind)


def setup_inputs(seed: int = 0) -> dict:
    seeds = jax.random.split(jax.random.key(seed), 8)
    tokens = scatter_about(seeds[0], (TOKENS, D), 1.0, 6.0, ((0, 8),))
    grad_out = scatter_about(seeds[1], (TOKENS, D), 1.0, 6.0, ((0, 8),))
    routes_keys = jax.random.split(jax.random.fold_in(seeds[2], 1), TOKENS // TOK_DEV)
    routes_turns = jax.random.permutation(jax.random.fold_in(seeds[2], 3), TOKENS // TOK_DEV)
    routes = jax.vmap(lambda own, number: routed_block(jax.random.fold_in(seeds[2], 2), own, number, TOK_DEV, EXPERTS, TOP, MOST, 2))(routes_keys, routes_turns).reshape((TOKENS, TOP))
    probs = jnp.clip(0.049804688 + 0.3486328 * jax.random.uniform(seeds[3], (TOKENS, TOP), jnp.float32) ** steps_of(seeds[3], (TOKENS, TOP), ((0, 8),), -0.2, 0.2), 0.049804688, 0.3984375).astype(jnp.bfloat16)
    w_gate = scatter_about(seeds[4], (EXPERTS, FF, D), D ** -0.5, 0.125, ((0, 8), (1, 4)))
    w_up = scatter_about(seeds[5], (EXPERTS, FF, D), D ** -0.5, 0.125, ((0, 8), (1, 4)))
    w_down = scatter_about(seeds[6], (EXPERTS, FF, D), FF ** -0.5, 0.21875, ((0, 8), (1, 4)))
    return dict(tokens=tokens, grad_out=grad_out, routes=routes, probs=probs, w_gate=w_gate, w_up=w_up, w_down=w_down)


def reference(tokens, grad_out, routes, probs, w_gate, w_up, w_down):
    expert_count = w_gate.shape[0]
    capacity = N_EXPERT * MOST
    pair_count = TOKENS * TOP
    shard_count = N_ETP
    flat_routes = routes.reshape(-1).astype(jnp.int32)
    sort_order = jnp.argsort(flat_routes, stable=True).astype(jnp.int32)
    ordered = flat_routes[sort_order]
    counts = jnp.zeros((expert_count,), jnp.int32).at[flat_routes].add(1)
    starts = jnp.cumsum(counts) - counts
    position = jnp.arange(pair_count, dtype=jnp.int32) - starts[ordered]
    slot_table = jnp.full((expert_count, capacity), pair_count, jnp.int32).at[ordered, position].set(sort_order)
    prob_flat = probs.reshape(-1)

    def expert_step(carried, inputs):
        grad_acc, prob_acc = carried
        index_row, gate_w, up_w, down_w = inputs
        filled = index_row < pair_count
        safe_index = jnp.where(filled, index_row, 0)
        token_of = safe_index // TOP
        row_vals = jnp.where(filled[:, None], tokens[token_of], 0)
        grad_vals = jnp.where(filled[:, None], grad_out[token_of], 0)
        weight = jnp.where(filled, prob_flat[safe_index], 0).astype(jnp.float32)[:, None]
        pre_gate = jnp.dot(row_vals, gate_w.T, preferred_element_type=jnp.float32)
        pre_up = jnp.dot(row_vals, up_w.T, preferred_element_type=jnp.float32)
        back_grad = jnp.dot(grad_vals, down_w.T, preferred_element_type=jnp.float32)
        sigma_gate = jax.nn.sigmoid(pre_gate)
        activated = pre_gate * sigma_gate
        hidden = (activated * pre_up).astype(jnp.bfloat16)
        prob_part = jnp.sum((hidden.astype(jnp.float32) * back_grad).reshape(capacity, shard_count, HID_DEV), axis=-1).astype(jnp.bfloat16)
        prob_vals = jnp.sum(prob_part.astype(jnp.float32), axis=1).astype(jnp.bfloat16)
        scaled = (weight * grad_vals.astype(jnp.float32)).astype(jnp.bfloat16)
        down_grad = jnp.dot(hidden.T, scaled, preferred_element_type=jnp.float32).astype(jnp.bfloat16)
        hidden_grad = weight * back_grad
        d_gate = (hidden_grad * pre_up * sigma_gate * (1.0 + pre_gate * (1.0 - sigma_gate))).astype(jnp.bfloat16)
        d_up = (hidden_grad * activated).astype(jnp.bfloat16)
        gate_grad = jnp.dot(d_gate.T, row_vals, preferred_element_type=jnp.float32).astype(jnp.bfloat16)
        up_grad = jnp.dot(d_up.T, row_vals, preferred_element_type=jnp.float32).astype(jnp.bfloat16)
        gate_parts = jnp.einsum("cgh,ghd->cgd", d_gate.astype(jnp.float32).reshape(capacity, shard_count, HID_DEV), gate_w.astype(jnp.float32).reshape(shard_count, HID_DEV, D))
        up_parts = jnp.einsum("cgh,ghd->cgd", d_up.astype(jnp.float32).reshape(capacity, shard_count, HID_DEV), up_w.astype(jnp.float32).reshape(shard_count, HID_DEV, D))
        row_part = (gate_parts + up_parts).astype(jnp.bfloat16)
        pair_grad = jnp.sum(row_part.astype(jnp.float32), axis=1).astype(jnp.bfloat16)
        token_target = jnp.where(filled, token_of, TOKENS)
        grad_acc = grad_acc.at[token_target].add(pair_grad.astype(jnp.float32), mode="drop")
        prob_acc = prob_acc.at[index_row].set(prob_vals, mode="drop")
        return (grad_acc, prob_acc), (gate_grad, up_grad, down_grad)

    initial = (jnp.zeros((TOKENS, D), jnp.float32), jnp.zeros((pair_count,), jnp.bfloat16))
    (grad_acc, prob_acc), (grad_gate, grad_up, grad_down) = lax.scan(expert_step, initial, (slot_table, w_gate, w_up, w_down))
    return grad_acc.astype(jnp.bfloat16), prob_acc.reshape(TOKENS, TOP), grad_gate, grad_up, grad_down
```

```python
import functools

import jax
import jax.numpy as jnp
from jax import lax
from jax.experimental import pallas as pl
from jax.experimental.pallas import tpu as pltpu
from jax.sharding import PartitionSpec as P

BF16 = jnp.bfloat16
F32 = jnp.float32
LANES = 128
VMEM_BYTES = 48 * 1024 * 1024


def token_sum(slot_rows, target, tok_rows, top_count):
    columns = slot_rows.shape[-1]
    picked = slot_rows.reshape(-1, columns)[target]
    return jnp.sum(picked.reshape(tok_rows, top_count, columns).astype(F32), axis=1).astype(BF16)


def expert_major(values, sources, local_experts, capacity):
    tail = values.shape[2:]
    shaped = values.reshape((sources, local_experts, capacity) + tail)
    order = (1, 0, 2) + tuple(range(3, 3 + len(tail)))
    return jnp.transpose(shaped, order).reshape((local_experts, sources * capacity) + tail)


def source_major(values, sources, local_experts, capacity):
    tail = values.shape[2:]
    shaped = values.reshape((local_experts, sources, capacity) + tail)
    order = (1, 0, 2) + tuple(range(3, 3 + len(tail)))
    return jnp.transpose(shaped, order).reshape((sources, local_experts * capacity) + tail)


def slots_of(tok_rows, top_count, expert_count):
    return max(2, 5 * tok_rows * top_count // (4 * expert_count))


def routed_body(tokens, grad_out, routes, probs, w_gate, w_up, w_down):
    sources = lax.axis_size("expert")
    local_experts = w_gate.shape[0]
    hid_units = w_gate.shape[1]
    expert_count = sources * local_experts
    tok_rows, top_count = routes.shape
    model_width = tokens.shape[1]
    capacity = slots_of(tok_rows, top_count, expert_count)
    pair_count = tok_rows * top_count
    flat_routes = routes.reshape(-1)
    one_hot = (flat_routes[:, None] == jnp.arange(expert_count, dtype=jnp.int32)[None, :]).astype(
        jnp.int32
    )
    slot_rank = jnp.sum(jnp.cumsum(one_hot, axis=0) * one_hot, axis=1) - 1
    target = flat_routes * capacity + slot_rank
    slot_table = (
        jnp.full((expert_count * capacity,), pair_count, jnp.int32)
        .at[target]
        .set(jnp.arange(pair_count, dtype=jnp.int32))
    )
    filled = slot_table < pair_count
    safe_index = jnp.where(filled, slot_table, 0)
    token_of = safe_index // top_count
    block_rows = local_experts * capacity
    send_prob = jnp.where(filled, probs.reshape(-1)[safe_index], 0).reshape(sources, block_rows)
    send_rows = jnp.where(filled[:, None], tokens[token_of], 0).reshape(
        sources, block_rows, model_width
    )
    send_grad = jnp.where(filled[:, None], grad_out[token_of], 0).reshape(
        sources, block_rows, model_width
    )
    recv_rows, recv_grad, recv_prob = (
        lax.all_to_all(send_rows, "expert", split_axis=0, concat_axis=0, tiled=True),
        lax.all_to_all(send_grad, "expert", split_axis=0, concat_axis=0, tiled=True),
        lax.all_to_all(send_prob, "expert", split_axis=0, concat_axis=0, tiled=True),
    )
    in_rows = expert_major(recv_rows, sources, local_experts, capacity)
    in_grad = expert_major(recv_grad, sources, local_experts, capacity)
    weight = expert_major(recv_prob, sources, local_experts, capacity).astype(F32)[..., None]
    gate_up = jnp.concatenate([w_gate, w_up], axis=1)
    both_pre = jnp.einsum("end,ehd->enh", in_rows, gate_up, preferred_element_type=F32)
    pre_gate = both_pre[..., :hid_units]
    pre_up = both_pre[..., hid_units:]
    back_grad = jnp.einsum("end,ehd->enh", in_grad, w_down, preferred_element_type=F32)
    sigma_gate = jax.nn.sigmoid(pre_gate)
    activated = pre_gate * sigma_gate
    hidden = (activated * pre_up).astype(BF16)
    prob_local = jnp.sum(hidden.astype(F32) * back_grad, axis=-1)
    prob_part = source_major(prob_local, sources, local_experts, capacity)
    scaled = (weight * in_grad.astype(F32)).astype(BF16)
    grad_down = jnp.einsum("enh,end->ehd", hidden, scaled, preferred_element_type=F32).astype(BF16)
    hidden_grad = weight * back_grad
    d_gate = (hidden_grad * pre_up * sigma_gate * (1.0 + pre_gate * (1.0 - sigma_gate))).astype(
        BF16
    )
    d_up = (hidden_grad * activated).astype(BF16)
    d_both = jnp.concatenate([d_gate, d_up], axis=-1)
    grad_both = jnp.einsum("enh,end->ehd", d_both, in_rows, preferred_element_type=F32).astype(BF16)
    grad_gate = grad_both[:, :hid_units]
    grad_up = grad_both[:, hid_units:]
    local_part = jnp.einsum("enh,ehd->end", d_both, gate_up, preferred_element_type=F32).astype(
        BF16
    )
    partial_sum = source_major(local_part, sources, local_experts, capacity).astype(F32)
    totals, prob_total = (
        lax.psum(partial_sum.astype(BF16), "etp").astype(F32),
        lax.psum(prob_part.astype(BF16), "etp").astype(F32),
    )
    back_rows, back_prob = (
        lax.all_to_all(totals.astype(BF16), "expert", split_axis=0, concat_axis=0, tiled=True),
        lax.all_to_all(prob_total.astype(BF16), "expert", split_axis=0, concat_axis=0, tiled=True),
    )
    grad_tokens = token_sum(back_rows, target, tok_rows, top_count)
    grad_probs = back_prob.reshape(-1)[target].reshape(tok_rows, top_count)
    return (grad_tokens, grad_probs, grad_gate, grad_up, grad_down)


def stage_kernel(local_experts, base_ref, *refs):
    (*chunks, gate_up, down, keep, send, rows, d_both, hid) = refs
    width = down.shape[1]
    units = down.shape[0]
    each = units // local_experts
    step = chunks[0].shape[0]
    for i, chunk in enumerate(chunks):
        rows[i * step : (i + 1) * step, :] = chunk[...]
    count = rows.shape[0]
    nt = (((1,), (1,)), ((), ()))
    pre = lax.dot_general(rows[:, :width], gate_up[...], nt, preferred_element_type=F32)
    back = lax.dot_general(rows[:, width : 2 * width], down[...], nt, preferred_element_type=F32)
    extra = rows[:, 2 * width :].astype(F32)
    lane = lax.broadcasted_iota(jnp.int32, extra.shape, 1)
    unit = lax.broadcasted_iota(jnp.int32, (count, units), 1)
    weight = jnp.zeros((count, units), F32)
    for e in range(local_experts):
        own = jnp.sum(jnp.where(lane == base_ref[0] + e, extra, 0.0), axis=1, keepdims=True)
        weight = jnp.where((unit >= e * each) & (unit < (e + 1) * each), own, weight)
    pre_gate = pre[:, :units]
    pre_up = pre[:, units:]
    sigma = 1.0 / (1.0 + jnp.exp(-pre_gate))
    activated = pre_gate * sigma
    hidden = (activated * pre_up).astype(BF16).astype(F32)
    product = hidden * back
    found = jnp.zeros(extra.shape, F32)
    for e in range(local_experts):
        mine = (unit >= e * each) & (unit < (e + 1) * each)
        own = jnp.sum(jnp.where(mine, product, 0.0), axis=1, keepdims=True)
        found = jnp.where(lane == base_ref[0] + e, own, found)
    hid[...] = (hidden * weight).astype(BF16)
    hidden_grad = weight * back
    d_both[:, :units] = (
        hidden_grad * pre_up * sigma * (1.0 + pre_gate * (1.0 - sigma))
    ).astype(BF16)
    d_both[:, units:] = (hidden_grad * activated).astype(BF16)
    part = jnp.dot(d_both[...], gate_up[...], preferred_element_type=F32).astype(BF16)
    half = count // 2
    keep[:, :width] = part[:half]
    send[:, :width] = part[half:]
    keep[:, width:] = found[:half].astype(BF16)
    send[:, width:] = found[half:].astype(BF16)


def stage(base, chunks, gate_up, down, local_experts):
    units, width = down.shape
    step, columns = chunks[0].shape
    count = step * len(chunks)
    extra = columns - 2 * width
    flops = 2 * count * width * (2 * units + units + 2 * units)
    return pl.pallas_call(
        functools.partial(stage_kernel, local_experts),
        out_shape=(
            jax.ShapeDtypeStruct((count // 2, width + extra), BF16),
            jax.ShapeDtypeStruct((count // 2, width + extra), BF16),
            jax.ShapeDtypeStruct((count, columns), BF16),
            jax.ShapeDtypeStruct((count, 2 * units), BF16),
            jax.ShapeDtypeStruct((count, units), BF16),
        ),
        in_specs=[pl.BlockSpec(memory_space=pltpu.SMEM)]
        + [pl.BlockSpec(memory_space=pltpu.VMEM)] * (len(chunks) + 2),
        out_specs=(pl.BlockSpec(memory_space=pltpu.VMEM),) * 5,
        compiler_params=pltpu.CompilerParams(vmem_limit_bytes=VMEM_BYTES),
        cost_estimate=pl.CostEstimate(
            flops=flops, bytes_accessed=4 * count * columns, transcendentals=count * units
        ),
        name="stage",
    )(base, *chunks, gate_up, down)


def weights_kernel(stages, *refs):
    ins = refs[: 4 * stages]
    gate, up, down = refs[4 * stages :]
    units = gate.shape[0]
    tn = (((0,), (0,)), ((), ()))
    both = 0.0
    below = 0.0
    for s in range(stages):
        x, o, d_both, hid = ins[4 * s : 4 * s + 4]
        both = both + lax.dot_general(d_both[...], x[...], tn, preferred_element_type=F32)
        below = below + lax.dot_general(hid[...], o[...], tn, preferred_element_type=F32)
    gate[...] = both[:units].astype(BF16)
    up[...] = both[units:].astype(BF16)
    down[...] = below.astype(BF16)


def weight_grads(parts, width, units):
    tile = 256
    tiles = width // tile
    specs, operands, total = [], [], 0
    for rows, d_both, hid in parts:
        count = rows.shape[0]
        total += count
        specs += [
            pl.BlockSpec((count, tile), lambda j: (0, j)),
            pl.BlockSpec((count, tile), lambda j: (0, j + tiles)),
            pl.BlockSpec(d_both.shape, lambda j: (0, 0)),
            pl.BlockSpec(hid.shape, lambda j: (0, 0)),
        ]
        operands += [rows, rows, d_both, hid]
    return pl.pallas_call(
        functools.partial(weights_kernel, len(parts)),
        grid=(tiles,),
        out_shape=(jax.ShapeDtypeStruct((units, width), BF16),) * 3,
        in_specs=specs,
        out_specs=(pl.BlockSpec((units, tile), lambda j: (0, j)),) * 3,
        compiler_params=pltpu.CompilerParams(vmem_limit_bytes=VMEM_BYTES),
        cost_estimate=pl.CostEstimate(
            flops=2 * total * width * 3 * units,
            bytes_accessed=4 * total * width + 6 * units * width,
            transcendentals=0,
        ),
        name="weight_grads",
    )(*operands)


def gathered_body(lines, tokens, grad_out, routes, probs, w_gate, w_up, w_down):
    axes = ("expert", "etp")
    local_experts, hid_units, width = w_gate.shape
    expert_count = 2 * lines * local_experts
    units = local_experts * hid_units
    tok_rows, top_count = routes.shape
    step = tok_rows // 4
    expert, etp = lax.axis_index("expert"), lax.axis_index("etp")
    side, core = etp // 2, etp % 2

    order = list(range(0, lines, 2)) + list(range(1, lines, 2))[::-1]
    after = {order[i]: order[(i + 1) % lines] for i in range(lines)}
    places = [
        (z, y, x, c) for z in range(lines) for y in range(2) for x in range(2) for c in range(2)
    ]

    def number(z, y, x, c):
        return ((z * 2 + y) * 2 + x) * 2 + c

    ring = [(number(z, y, x, c), number(after[z], y, x, c)) for z, y, x, c in places]
    over_y = [(number(z, y, x, c), number(z, 1 - y, x, c)) for z, y, x, c in places]
    over_x = [(number(z, y, x, c), number(z, y, 1 - x, c)) for z, y, x, c in places]
    over_c = [(number(z, y, x, c), number(z, y, x, 1 - c)) for z, y, x, c in places]

    def move(value, pairs):
        return lax.ppermute(value, axes, pairs)

    extra = -(-expert_count // LANES) * LANES
    named = routes[:, :, None] == jnp.arange(extra, dtype=jnp.int32)
    dense = jnp.sum(jnp.where(named, probs[:, :, None], 0).astype(F32), axis=1).astype(BF16)
    block = jnp.concatenate([tokens, grad_out, dense], axis=1).reshape(4, step, -1)

    def quarter(x, c):
        return lax.dynamic_index_in_dim(block, 2 * x + c, 0, keepdims=False)

    here = quarter(side, core)
    gate_up = jnp.concatenate([w_gate.reshape(units, width), w_up.reshape(units, width)], axis=0)
    down = w_down.reshape(units, width)
    base = (expert * local_experts).astype(jnp.int32).reshape(1)

    line = [here]
    for s in range(1, lines):
        line.append(move(line[-1], ring))
    other = [move(v, over_y) for v in line]
    line_x = [quarter(1 - side, core)] + [move(v, over_x) for v in line[1:]]
    other_x = [move(v, over_x) for v in other]
    parts, sums = [], []
    for s in range(lines):
        mine = [line[s], line_x[s], other[s], other_x[s]]
        if s == 0:
            theirs = [quarter(side, 1 - core), quarter(1 - side, 1 - core)] + [
                move(v, over_c) for v in mine[2:]
            ]
        else:
            theirs = [move(v, over_c) for v in mine]
        keep, send, rows, d_both, hid = stage(base, mine + theirs, gate_up, down, local_experts)
        parts.append((rows, d_both, hid))
        chip = keep.astype(F32) + move(send, over_c).astype(F32)
        far = move(chip[2 * step :].astype(BF16), over_y)
        sums.append(chip[: 2 * step] + far.astype(F32))
    total = sums[1]
    for s in list(range(2, lines)) + [0]:
        total = sums[s] + move(total.astype(BF16), ring).astype(F32)
    total = total.astype(BF16)
    cross = move(total, over_x)
    final = (
        total.astype(F32) + jnp.concatenate([cross[step:], cross[:step]], axis=0).astype(F32)
    ).astype(BF16)
    beside = move(final, over_c)
    grad_gate, grad_up, grad_down = weight_grads(parts, width, units)

    pair = jnp.stack([final, beside]).reshape(2, 2, step, -1)
    pair = jnp.where(core == 0, pair, pair[::-1])
    pair = jnp.where(side == 0, pair, pair[:, ::-1])
    whole = jnp.transpose(pair, (1, 0, 2, 3)).reshape(tok_rows, -1)
    grad_tokens = whole[:, :width]
    found = whole[:, None, width:]
    grad_probs = jnp.sum(jnp.where(named, found, 0).astype(F32), axis=2).astype(BF16)
    shape = w_gate.shape
    return (
        grad_tokens,
        grad_probs,
        grad_gate.reshape(shape),
        grad_up.reshape(shape),
        grad_down.reshape(shape),
    )


def body(sources, splits, tokens, grad_out, routes, probs, w_gate, w_up, w_down):
    tok_rows, top_count = routes.shape
    local_experts = w_gate.shape[0]
    slots = local_experts * slots_of(tok_rows, top_count, sources * local_experts)
    fits = splits == 4 and sources % 2 == 0 and sources >= 4 and tok_rows % 64 == 0
    args = (tokens, grad_out, routes, probs, w_gate, w_up, w_down)
    if fits and slots >= tok_rows:
        return gathered_body(sources // 2, *args)
    return routed_body(*args)


def solution(mesh):
    return jax.shard_map(
        functools.partial(body, mesh.shape["expert"], mesh.shape["etp"]),
        mesh=mesh,
        in_specs=(
            P("expert", None),
            P("expert", None),
            P("expert", None),
            P("expert", None),
            P("expert", "etp", None),
            P("expert", "etp", None),
            P("expert", "etp", None),
        ),
        out_specs=(
            P("expert", None),
            P("expert", None),
            P("expert", "etp", None),
            P("expert", "etp", None),
            P("expert", "etp", None),
        ),
        check_vma=False,
    )
```

```python
import functools

import jax
import jax.numpy as jnp
from jax import lax
from jax.experimental import pallas as pl
from jax.experimental.pallas import tpu as pltpu
from jax.sharding import PartitionSpec as P

BF16 = jnp.bfloat16
F32 = jnp.float32
LANES = 128
VMEM_BYTES = 16 * 1024 * 1024


def token_sum(slot_rows, target, tok_rows, top_count):
    columns = slot_rows.shape[-1]
    picked = slot_rows.reshape(-1, columns)[target]
    return jnp.sum(picked.reshape(tok_rows, top_count, columns).astype(F32), axis=1).astype(BF16)


def expert_major(values, sources, local_experts, capacity):
    tail = values.shape[2:]
    shaped = values.reshape((sources, local_experts, capacity) + tail)
    order = (1, 0, 2) + tuple(range(3, 3 + len(tail)))
    return jnp.transpose(shaped, order).reshape((local_experts, sources * capacity) + tail)


def source_major(values, sources, local_experts, capacity):
    tail = values.shape[2:]
    shaped = values.reshape((local_experts, sources, capacity) + tail)
    order = (1, 0, 2) + tuple(range(3, 3 + len(tail)))
    return jnp.transpose(shaped, order).reshape((sources, local_experts * capacity) + tail)


def slots_of(tok_rows, top_count, expert_count):
    return max(2, 5 * tok_rows * top_count // (4 * expert_count))


def routed_body(tokens, grad_out, routes, probs, w_gate, w_up, w_down):
    sources = lax.axis_size("expert")
    local_experts = w_gate.shape[0]
    hid_units = w_gate.shape[1]
    expert_count = sources * local_experts
    tok_rows, top_count = routes.shape
    model_width = tokens.shape[1]
    capacity = slots_of(tok_rows, top_count, expert_count)
    pair_count = tok_rows * top_count
    flat_routes = routes.reshape(-1)
    one_hot = (flat_routes[:, None] == jnp.arange(expert_count, dtype=jnp.int32)[None, :]).astype(
        jnp.int32
    )
    slot_rank = jnp.sum(jnp.cumsum(one_hot, axis=0) * one_hot, axis=1) - 1
    target = flat_routes * capacity + slot_rank
    slot_table = (
        jnp.full((expert_count * capacity,), pair_count, jnp.int32)
        .at[target]
        .set(jnp.arange(pair_count, dtype=jnp.int32))
    )
    filled = slot_table < pair_count
    safe_index = jnp.where(filled, slot_table, 0)
    token_of = safe_index // top_count
    block_rows = local_experts * capacity
    send_prob = jnp.where(filled, probs.reshape(-1)[safe_index], 0).reshape(sources, block_rows)
    send_rows = jnp.where(filled[:, None], tokens[token_of], 0).reshape(
        sources, block_rows, model_width
    )
    send_grad = jnp.where(filled[:, None], grad_out[token_of], 0).reshape(
        sources, block_rows, model_width
    )
    recv_rows, recv_grad, recv_prob = (
        lax.all_to_all(send_rows, "expert", split_axis=0, concat_axis=0, tiled=True),
        lax.all_to_all(send_grad, "expert", split_axis=0, concat_axis=0, tiled=True),
        lax.all_to_all(send_prob, "expert", split_axis=0, concat_axis=0, tiled=True),
    )
    in_rows = expert_major(recv_rows, sources, local_experts, capacity)
    in_grad = expert_major(recv_grad, sources, local_experts, capacity)
    weight = expert_major(recv_prob, sources, local_experts, capacity).astype(F32)[..., None]
    gate_up = jnp.concatenate([w_gate, w_up], axis=1)
    both_pre = jnp.einsum("end,ehd->enh", in_rows, gate_up, preferred_element_type=F32)
    pre_gate = both_pre[..., :hid_units]
    pre_up = both_pre[..., hid_units:]
    back_grad = jnp.einsum("end,ehd->enh", in_grad, w_down, preferred_element_type=F32)
    sigma_gate = jax.nn.sigmoid(pre_gate)
    activated = pre_gate * sigma_gate
    hidden = (activated * pre_up).astype(BF16)
    prob_local = jnp.sum(hidden.astype(F32) * back_grad, axis=-1)
    prob_part = source_major(prob_local, sources, local_experts, capacity)
    scaled = (weight * in_grad.astype(F32)).astype(BF16)
    grad_down = jnp.einsum("enh,end->ehd", hidden, scaled, preferred_element_type=F32).astype(BF16)
    hidden_grad = weight * back_grad
    d_gate = (hidden_grad * pre_up * sigma_gate * (1.0 + pre_gate * (1.0 - sigma_gate))).astype(
        BF16
    )
    d_up = (hidden_grad * activated).astype(BF16)
    d_both = jnp.concatenate([d_gate, d_up], axis=-1)
    grad_both = jnp.einsum("enh,end->ehd", d_both, in_rows, preferred_element_type=F32).astype(BF16)
    grad_gate = grad_both[:, :hid_units]
    grad_up = grad_both[:, hid_units:]
    local_part = jnp.einsum("enh,ehd->end", d_both, gate_up, preferred_element_type=F32).astype(
        BF16
    )
    partial_sum = source_major(local_part, sources, local_experts, capacity).astype(F32)
    totals, prob_total = (
        lax.psum(partial_sum.astype(BF16), "etp").astype(F32),
        lax.psum(prob_part.astype(BF16), "etp").astype(F32),
    )
    back_rows, back_prob = (
        lax.all_to_all(totals.astype(BF16), "expert", split_axis=0, concat_axis=0, tiled=True),
        lax.all_to_all(prob_total.astype(BF16), "expert", split_axis=0, concat_axis=0, tiled=True),
    )
    grad_tokens = token_sum(back_rows, target, tok_rows, top_count)
    grad_probs = back_prob.reshape(-1)[target].reshape(tok_rows, top_count)
    return (grad_tokens, grad_probs, grad_gate, grad_up, grad_down)


def stage_kernel(local_experts, base_ref, mine, theirs, gate_up, down, keep, send, d_both, hid):
    units, width = down.shape
    each = units // local_experts
    half = mine.shape[0]
    count = 2 * half
    nt = (((1,), (1,)), ((), ()))

    def both(start, stop):
        return jnp.concatenate([mine[:, start:stop], theirs[:, start:stop]], axis=0)

    pre = lax.dot_general(both(0, width), gate_up[...], nt, preferred_element_type=F32)
    back = lax.dot_general(both(width, 2 * width), down[...], nt, preferred_element_type=F32)
    extra = both(2 * width, mine.shape[1]).astype(F32)
    lane = lax.broadcasted_iota(jnp.int32, extra.shape, 1)
    unit = lax.broadcasted_iota(jnp.int32, (count, units), 1)
    weight = jnp.zeros((count, units), F32)
    for e in range(local_experts):
        own = jnp.sum(jnp.where(lane == base_ref[0] + e, extra, 0.0), axis=1, keepdims=True)
        weight = jnp.where((unit >= e * each) & (unit < (e + 1) * each), own, weight)
    pre_gate = pre[:, :units]
    pre_up = pre[:, units:]
    sigma = 1.0 / (1.0 + jnp.exp(-pre_gate))
    activated = pre_gate * sigma
    hidden = (activated * pre_up).astype(BF16).astype(F32)
    product = hidden * back
    found = jnp.zeros(extra.shape, F32)
    for e in range(local_experts):
        covered = (unit >= e * each) & (unit < (e + 1) * each)
        own = jnp.sum(jnp.where(covered, product, 0.0), axis=1, keepdims=True)
        found = jnp.where(lane == base_ref[0] + e, own, found)
    hid[...] = (hidden * weight).astype(BF16)
    hidden_grad = weight * back
    d_both[:, :units] = (
        hidden_grad * pre_up * sigma * (1.0 + pre_gate * (1.0 - sigma))
    ).astype(BF16)
    d_both[:, units:] = (hidden_grad * activated).astype(BF16)
    part = jnp.dot(d_both[...], gate_up[...], preferred_element_type=F32).astype(BF16)
    keep[:, :width] = part[:half]
    send[:, :width] = part[half:]
    keep[:, width:] = found[:half].astype(BF16)
    send[:, width:] = found[half:].astype(BF16)


def stage(base, mine, theirs, gate_up, down, local_experts):
    units, width = down.shape
    half, columns = mine.shape
    count = 2 * half
    extra = columns - 2 * width
    flops = 2 * count * width * (2 * units + units + 2 * units)
    return pl.pallas_call(
        functools.partial(stage_kernel, local_experts),
        out_shape=(
            jax.ShapeDtypeStruct((half, width + extra), BF16),
            jax.ShapeDtypeStruct((half, width + extra), BF16),
            jax.ShapeDtypeStruct((count, 2 * units), BF16),
            jax.ShapeDtypeStruct((count, units), BF16),
        ),
        in_specs=[pl.BlockSpec(memory_space=pltpu.SMEM)]
        + [pl.BlockSpec(memory_space=pltpu.VMEM)] * 4,
        out_specs=(pl.BlockSpec(memory_space=pltpu.VMEM),) * 4,
        compiler_params=pltpu.CompilerParams(vmem_limit_bytes=VMEM_BYTES),
        cost_estimate=pl.CostEstimate(
            flops=flops, bytes_accessed=4 * count * columns, transcendentals=count * units
        ),
        name="stage",
    )(base, mine, theirs, gate_up, down)


def weights_kernel(stages, *refs):
    out = refs[-1]
    tn = (((0,), (0,)), ((), ()))
    total = 0.0
    for s in range(stages):
        mine, theirs, hid = refs[3 * s : 3 * s + 3]
        rows = jnp.concatenate([mine[...], theirs[...]], axis=0)
        total = total + lax.dot_general(hid[...], rows, tn, preferred_element_type=F32)
    out[...] = total.astype(BF16)


def weight_grads(parts, side, width, units, which=0):
    tile = 512
    tiles = width // tile
    specs, operands, total = [], [], 0
    for mine, theirs, hid in parts:
        half = mine.shape[0]
        total += 2 * half
        specs += [pl.BlockSpec((half, tile), lambda j: (0, j + side * tiles))] * 2
        specs += [pl.BlockSpec((2 * half, units), lambda j: (0, which))]
        operands += [pltpu.with_memory_space_constraint(v, pltpu.HBM) for v in (mine, theirs, hid)]
    return pl.pallas_call(
        functools.partial(weights_kernel, len(parts)),
        grid=(tiles,),
        out_shape=jax.ShapeDtypeStruct((units, width), BF16),
        in_specs=specs,
        out_specs=pl.BlockSpec((units, tile), lambda j: (0, j)),
        compiler_params=pltpu.CompilerParams(vmem_limit_bytes=VMEM_BYTES),
        cost_estimate=pl.CostEstimate(
            flops=2 * total * width * units,
            bytes_accessed=2 * total * width + 2 * units * width,
            transcendentals=0,
        ),
        name="weight_grads",
    )(*operands)


def pack_kernel(
    step, quarters, routes, probs, tokens, grad_out, *refs
):
    outs, (dense, sem) = refs[:4], refs[4:]
    width = tokens.shape[1]
    copies = []
    for i, out in enumerate(outs):
        place = pl.ds(pl.multiple_of(quarters[i] * step, step), step)
        copies.append(
            pltpu.make_async_copy(tokens.at[place, :], out.at[:, pl.ds(0, width)], sem.at[2 * i])
        )
        copies.append(
            pltpu.make_async_copy(
                grad_out.at[place, :], out.at[:, pl.ds(width, width)], sem.at[2 * i + 1]
            )
        )
    for copy in copies:
        copy.start()
    named = routes[...]
    given = probs[...].astype(F32)
    lanes = dense.shape[1]
    ids = lax.broadcasted_iota(jnp.int32, (lanes, named.shape[1]), 0)
    spread = jnp.zeros(ids.shape, F32)
    for k in range(named.shape[0]):
        spread = spread + jnp.where(ids == named[k : k + 1, :], given[k : k + 1, :], 0.0)
    dense[...] = spread.T
    for copy in copies:
        copy.wait()
    for i, out in enumerate(outs):
        place = pl.ds(pl.multiple_of(quarters[i] * step, step), step)
        out[:, 2 * width :] = dense[place, :].astype(BF16)


def pack(quarters, routes, probs, tokens, grad_out, lanes):
    rows, width = tokens.shape
    step = rows // 4
    return pl.pallas_call(
        functools.partial(pack_kernel, step),
        out_shape=(jax.ShapeDtypeStruct((step, 2 * width + lanes), BF16),) * 4,
        in_specs=[pl.BlockSpec(memory_space=pltpu.SMEM)]
        + [pl.BlockSpec(memory_space=pltpu.VMEM)] * 2
        + [pl.BlockSpec(memory_space=pltpu.HBM)] * 2,
        out_specs=(pl.BlockSpec(memory_space=pltpu.VMEM),) * 4,
        scratch_shapes=[pltpu.VMEM((rows, lanes), F32), pltpu.SemaphoreType.DMA((8,))],
        name="pack",
    )(quarters, routes.T, probs.T, tokens, grad_out)


def after(value, *others):
    return lax.optimization_barrier((value, *others))[0] if others else value


def gathered_body(tokens, grad_out, routes, probs, w_gate, w_up, w_down):
    lines = 4
    axes = ("expert", "etp")
    local_experts, hid_units, width = w_gate.shape
    expert_count = 2 * lines * local_experts
    units = local_experts * hid_units
    tok_rows, top_count = routes.shape
    step = tok_rows // 4
    expert, etp = lax.axis_index("expert"), lax.axis_index("etp")
    side, core = etp // 2, etp % 2

    order = (0, 2, 3, 1)
    places = [
        (z, y, x, c) for z in range(lines) for y in range(2) for x in range(2) for c in range(2)
    ]

    def number(z, y, x, c):
        return ((z * 2 + y) * 2 + x) * 2 + c

    def along(hops):
        ahead = {order[i]: order[(i + hops) % lines] for i in range(lines)}
        return [(number(z, y, x, c), number(ahead[z], y, x, c)) for z, y, x, c in places]

    over_y = [(number(z, y, x, c), number(z, 1 - y, x, c)) for z, y, x, c in places]
    over_x = [(number(z, y, x, c), number(z, y, 1 - x, c)) for z, y, x, c in places]
    over_c = [(number(z, y, x, c), number(z, y, x, 1 - c)) for z, y, x, c in places]

    def move(value, pairs):
        return lax.ppermute(value, axes, pairs)

    extra = -(-expert_count // LANES) * LANES
    ids = jnp.arange(extra, dtype=jnp.int32)

    quarters = jnp.stack(
        [2 * x + c for x, c in ((side, core), (1 - side, core), (side, 1 - core), (1 - side, 1 - core))]
    ).astype(jnp.int32)
    here, near, *rest = pack(quarters, routes, probs, tokens, grad_out, extra)
    gate_up = jnp.concatenate([w_gate.reshape(units, width), w_up.reshape(units, width)], axis=0)
    down = w_down.reshape(units, width)
    base = (expert * local_experts).astype(jnp.int32).reshape(1)

    line = {0: here, 1: move(here, along(1)), }
    line[3] = move(after(here, line[1]), along(-1))
    other, line_x, other_x = {0: move(here, over_y)}, {0: near}, {0: move(near, over_y)}
    line_x[1] = move(line[1], over_x)
    line[2] = move(line[1], along(1))
    for s in (1, 3, 2):
        other[s] = move(line[s], over_y)

    pairs = [
        move(jnp.concatenate(v, axis=0), over_x)
        for v in ([other[1], line[3]], [line[2], other[2]])
    ]
    rows, grads, chips, fars, backs = {}, {}, {}, {}, {}
    sequence = list(range(lines))
    for s in sequence:
        if s == 0:
            other_x[0] = after(other_x[0], line[2])
        mine = jnp.concatenate([line[s], line_x[s], other[s], other_x[s]], axis=0)
        if s == 0:
            theirs = jnp.concatenate(rest + [move(mine[2 * step :], over_c)], axis=0)
        else:
            theirs = move(mine, over_c)
        wait = [chips[s - 1]] if s else []
        outs = stage(after(base, *wait), mine, theirs, gate_up, down, local_experts)
        if s == 0:
            outs, pair, other[3] = lax.optimization_barrier((outs, pairs[0], other[3]))
            other_x[1], line_x[3] = pair[:step], pair[step:]
        elif s == 1:
            outs, pair, fars[0] = lax.optimization_barrier((outs, pairs[1], fars[0]))
            line_x[2], other_x[2] = pair[:step], pair[step:]
            other_x[3] = move(other[3], over_x)
        elif s == 2:
            outs, other_x[3], fars[1] = lax.optimization_barrier((outs, other_x[3], fars[1]))
            backs[1] = move((chips[1][: 2 * step] + fars[1].astype(F32)).astype(BF16), along(-1))
        else:
            outs, fars[2], backs[1] = lax.optimization_barrier((outs, fars[2], backs[1]))
        keep, send, d_both, hid = outs
        rows[s], grads[s] = (mine, theirs), (d_both, hid)
        chips[s] = keep.astype(F32) + move(send, over_c).astype(F32)
        fars[s] = move(chips[s][2 * step :].astype(BF16), over_y)
    hids = [rows[s] + (grads[s][1],) for s in sequence]
    boths = [rows[s] + (grads[s][0],) for s in sequence]
    held = chips[2][: 2 * step] + fars[2].astype(F32)
    passed = move(held.astype(BF16), along(1))
    hids[-1] = hids[-1][:2] + (after(hids[-1][2], held, chips[3]),)
    grad_down = weight_grads(hids, 1, width, units)
    grad_down, fars[3], passed = lax.optimization_barrier((grad_down, fars[3], passed))
    held = chips[3][: 2 * step] + fars[3].astype(F32) + passed.astype(F32)
    backs[3] = move(held.astype(BF16), along(1))
    boths[-1] = boths[-1][:2] + (after(boths[-1][2], grad_down, held),)
    grad_gate = weight_grads(boths, 0, width, units)
    grad_gate, backs[3] = lax.optimization_barrier((grad_gate, backs[3]))
    total = chips[0][: 2 * step] + fars[0].astype(F32)
    for back in backs.values():
        total = total + back.astype(F32)
    total = total.astype(BF16)
    cross = move(total, over_x)
    boths[-1] = boths[-1][:2] + (after(boths[-1][2], total),)
    grad_up = weight_grads(boths, 0, width, units, 1)
    grad_up, cross = lax.optimization_barrier((grad_up, cross))
    final = (
        total.astype(F32) + jnp.concatenate([cross[step:], cross[:step]], axis=0).astype(F32)
    ).astype(BF16)
    beside = move(final, over_c)

    pair = jnp.stack([final, beside]).reshape(2, 2, step, -1)
    pair = jnp.where(core == 0, pair, pair[::-1])
    pair = jnp.where(side == 0, pair, pair[:, ::-1])
    whole = jnp.transpose(pair, (1, 0, 2, 3)).reshape(tok_rows, -1)
    grad_tokens = whole[:, :width]
    found = whole[:, None, width:]
    named = routes[:, :, None] == ids
    grad_probs = jnp.sum(jnp.where(named, found, 0).astype(F32), axis=2).astype(BF16)
    shape = w_gate.shape
    return (
        grad_tokens,
        grad_probs,
        grad_gate.reshape(shape),
        grad_up.reshape(shape),
        grad_down.reshape(shape),
    )


def body(sources, splits, tokens, grad_out, routes, probs, w_gate, w_up, w_down):
    tok_rows, top_count = routes.shape
    local_experts = w_gate.shape[0]
    slots = local_experts * slots_of(tok_rows, top_count, sources * local_experts)
    fits = splits == 4 and sources == 8 and tok_rows % 64 == 0
    args = (tokens, grad_out, routes, probs, w_gate, w_up, w_down)
    if fits and slots >= tok_rows:
        return gathered_body(*args)
    return routed_body(*args)


def solution(mesh):
    return jax.shard_map(
        functools.partial(body, mesh.shape["expert"], mesh.shape["etp"]),
        mesh=mesh,
        in_specs=(
            P("expert", None),
            P("expert", None),
            P("expert", None),
            P("expert", None),
            P("expert", "etp", None),
            P("expert", "etp", None),
            P("expert", "etp", None),
        ),
        out_specs=(
            P("expert", None),
            P("expert", None),
            P("expert", "etp", None),
            P("expert", "etp", None),
            P("expert", "etp", None),
        ),
        check_vma=False,
    )
```

```python
import functools

import jax
import jax.numpy as jnp
from jax import lax
from jax.experimental import pallas as pl
from jax.experimental.pallas import tpu as pltpu
from jax.sharding import PartitionSpec as P

BF16 = jnp.bfloat16
F32 = jnp.float32
LANES = 128
VMEM_BYTES = 16 * 1024 * 1024


def token_sum(slot_rows, target, tok_rows, top_count):
    columns = slot_rows.shape[-1]
    picked = slot_rows.reshape(-1, columns)[target]
    return jnp.sum(picked.reshape(tok_rows, top_count, columns).astype(F32), axis=1).astype(BF16)


def expert_major(values, sources, local_experts, capacity):
    tail = values.shape[2:]
    shaped = values.reshape((sources, local_experts, capacity) + tail)
    order = (1, 0, 2) + tuple(range(3, 3 + len(tail)))
    return jnp.transpose(shaped, order).reshape((local_experts, sources * capacity) + tail)


def source_major(values, sources, local_experts, capacity):
    tail = values.shape[2:]
    shaped = values.reshape((local_experts, sources, capacity) + tail)
    order = (1, 0, 2) + tuple(range(3, 3 + len(tail)))
    return jnp.transpose(shaped, order).reshape((sources, local_experts * capacity) + tail)


def slots_of(tok_rows, top_count, expert_count):
    return max(2, 5 * tok_rows * top_count // (4 * expert_count))


def routed_body(tokens, grad_out, routes, probs, w_gate, w_up, w_down):
    sources = lax.axis_size("expert")
    local_experts = w_gate.shape[0]
    hid_units = w_gate.shape[1]
    expert_count = sources * local_experts
    tok_rows, top_count = routes.shape
    model_width = tokens.shape[1]
    capacity = slots_of(tok_rows, top_count, expert_count)
    pair_count = tok_rows * top_count
    flat_routes = routes.reshape(-1)
    one_hot = (flat_routes[:, None] == jnp.arange(expert_count, dtype=jnp.int32)[None, :]).astype(
        jnp.int32
    )
    slot_rank = jnp.sum(jnp.cumsum(one_hot, axis=0) * one_hot, axis=1) - 1
    target = flat_routes * capacity + slot_rank
    slot_table = (
        jnp.full((expert_count * capacity,), pair_count, jnp.int32)
        .at[target]
        .set(jnp.arange(pair_count, dtype=jnp.int32))
    )
    filled = slot_table < pair_count
    safe_index = jnp.where(filled, slot_table, 0)
    token_of = safe_index // top_count
    block_rows = local_experts * capacity
    send_prob = jnp.where(filled, probs.reshape(-1)[safe_index], 0).reshape(sources, block_rows)
    send_rows = jnp.where(filled[:, None], tokens[token_of], 0).reshape(
        sources, block_rows, model_width
    )
    send_grad = jnp.where(filled[:, None], grad_out[token_of], 0).reshape(
        sources, block_rows, model_width
    )
    recv_rows, recv_grad, recv_prob = (
        lax.all_to_all(send_rows, "expert", split_axis=0, concat_axis=0, tiled=True),
        lax.all_to_all(send_grad, "expert", split_axis=0, concat_axis=0, tiled=True),
        lax.all_to_all(send_prob, "expert", split_axis=0, concat_axis=0, tiled=True),
    )
    in_rows = expert_major(recv_rows, sources, local_experts, capacity)
    in_grad = expert_major(recv_grad, sources, local_experts, capacity)
    weight = expert_major(recv_prob, sources, local_experts, capacity).astype(F32)[..., None]
    gate_up = jnp.concatenate([w_gate, w_up], axis=1)
    both_pre = jnp.einsum("end,ehd->enh", in_rows, gate_up, preferred_element_type=F32)
    pre_gate = both_pre[..., :hid_units]
    pre_up = both_pre[..., hid_units:]
    back_grad = jnp.einsum("end,ehd->enh", in_grad, w_down, preferred_element_type=F32)
    sigma_gate = jax.nn.sigmoid(pre_gate)
    activated = pre_gate * sigma_gate
    hidden = (activated * pre_up).astype(BF16)
    prob_local = jnp.sum(hidden.astype(F32) * back_grad, axis=-1)
    prob_part = source_major(prob_local, sources, local_experts, capacity)
    scaled = (weight * in_grad.astype(F32)).astype(BF16)
    grad_down = jnp.einsum("enh,end->ehd", hidden, scaled, preferred_element_type=F32).astype(BF16)
    hidden_grad = weight * back_grad
    d_gate = (hidden_grad * pre_up * sigma_gate * (1.0 + pre_gate * (1.0 - sigma_gate))).astype(
        BF16
    )
    d_up = (hidden_grad * activated).astype(BF16)
    d_both = jnp.concatenate([d_gate, d_up], axis=-1)
    grad_both = jnp.einsum("enh,end->ehd", d_both, in_rows, preferred_element_type=F32).astype(BF16)
    grad_gate = grad_both[:, :hid_units]
    grad_up = grad_both[:, hid_units:]
    local_part = jnp.einsum("enh,ehd->end", d_both, gate_up, preferred_element_type=F32).astype(
        BF16
    )
    partial_sum = source_major(local_part, sources, local_experts, capacity).astype(F32)
    totals, prob_total = (
        lax.psum(partial_sum.astype(BF16), "etp").astype(F32),
        lax.psum(prob_part.astype(BF16), "etp").astype(F32),
    )
    back_rows, back_prob = (
        lax.all_to_all(totals.astype(BF16), "expert", split_axis=0, concat_axis=0, tiled=True),
        lax.all_to_all(prob_total.astype(BF16), "expert", split_axis=0, concat_axis=0, tiled=True),
    )
    grad_tokens = token_sum(back_rows, target, tok_rows, top_count)
    grad_probs = back_prob.reshape(-1)[target].reshape(tok_rows, top_count)
    return (grad_tokens, grad_probs, grad_gate, grad_up, grad_down)


def stage_kernel(local_experts, base_ref, mine, theirs, gate_up, down, keep, send, d_both, hid):
    units, width = down.shape
    each = units // local_experts
    half = mine.shape[0]
    count = 2 * half
    nt = (((1,), (1,)), ((), ()))

    def both(start, stop):
        return jnp.concatenate([mine[:, start:stop], theirs[:, start:stop]], axis=0)

    pre = lax.dot_general(both(0, width), gate_up[...], nt, preferred_element_type=F32)
    back = lax.dot_general(both(width, 2 * width), down[...], nt, preferred_element_type=F32)
    extra = both(2 * width, mine.shape[1]).astype(F32)
    lane = lax.broadcasted_iota(jnp.int32, extra.shape, 1)
    unit = lax.broadcasted_iota(jnp.int32, (count, units), 1)
    weight = jnp.zeros((count, units), F32)
    for e in range(local_experts):
        own = jnp.sum(jnp.where(lane == base_ref[0] + e, extra, 0.0), axis=1, keepdims=True)
        weight = jnp.where((unit >= e * each) & (unit < (e + 1) * each), own, weight)
    pre_gate = pre[:, :units]
    pre_up = pre[:, units:]
    sigma = 1.0 / (1.0 + jnp.exp(-pre_gate))
    activated = pre_gate * sigma
    hidden = (activated * pre_up).astype(BF16).astype(F32)
    product = hidden * back
    found = jnp.zeros(extra.shape, F32)
    for e in range(local_experts):
        covered = (unit >= e * each) & (unit < (e + 1) * each)
        own = jnp.sum(jnp.where(covered, product, 0.0), axis=1, keepdims=True)
        found = jnp.where(lane == base_ref[0] + e, own, found)
    hid[...] = (hidden * weight).astype(BF16)
    hidden_grad = weight * back
    d_both[:, :units] = (
        hidden_grad * pre_up * sigma * (1.0 + pre_gate * (1.0 - sigma))
    ).astype(BF16)
    d_both[:, units:] = (hidden_grad * activated).astype(BF16)
    part = jnp.dot(d_both[...], gate_up[...], preferred_element_type=F32).astype(BF16)
    keep[:, :width] = part[:half]
    send[:, :width] = part[half:]
    keep[:, width:] = found[:half].astype(BF16)
    send[:, width:] = found[half:].astype(BF16)


def stage(base, mine, theirs, gate_up, down, local_experts):
    units, width = down.shape
    half, columns = mine.shape
    count = 2 * half
    extra = columns - 2 * width
    flops = 2 * count * width * (2 * units + units + 2 * units)
    return pl.pallas_call(
        functools.partial(stage_kernel, local_experts),
        out_shape=(
            jax.ShapeDtypeStruct((half, width + extra), BF16),
            jax.ShapeDtypeStruct((half, width + extra), BF16),
            jax.ShapeDtypeStruct((count, 2 * units), BF16),
            jax.ShapeDtypeStruct((count, units), BF16),
        ),
        in_specs=[pl.BlockSpec(memory_space=pltpu.SMEM)]
        + [pl.BlockSpec(memory_space=pltpu.VMEM)] * 4,
        out_specs=(pl.BlockSpec(memory_space=pltpu.VMEM),) * 4,
        compiler_params=pltpu.CompilerParams(vmem_limit_bytes=VMEM_BYTES),
        cost_estimate=pl.CostEstimate(
            flops=flops, bytes_accessed=4 * count * columns, transcendentals=count * units
        ),
        name="stage",
    )(base, mine, theirs, gate_up, down)


def weights_kernel(stages, *refs):
    out = refs[-1]
    tn = (((0,), (0,)), ((), ()))
    total = 0.0
    for s in range(stages):
        mine, theirs, hid = refs[3 * s : 3 * s + 3]
        rows = jnp.concatenate([mine[...], theirs[...]], axis=0)
        total = total + lax.dot_general(hid[...], rows, tn, preferred_element_type=F32)
    out[...] = total.astype(BF16)


def weight_grads(parts, side, width, units, which=0):
    tile = 512
    tiles = width // tile
    specs, operands, total = [], [], 0
    for mine, theirs, hid in parts:
        half = mine.shape[0]
        total += 2 * half
        specs += [pl.BlockSpec((half, tile), lambda j: (0, j + side * tiles))] * 2
        specs += [pl.BlockSpec((2 * half, units), lambda j: (0, which))]
        operands += [pltpu.with_memory_space_constraint(v, pltpu.HBM) for v in (mine, theirs, hid)]
    return pl.pallas_call(
        functools.partial(weights_kernel, len(parts)),
        grid=(tiles,),
        out_shape=jax.ShapeDtypeStruct((units, width), BF16),
        in_specs=specs,
        out_specs=pl.BlockSpec((units, tile), lambda j: (0, j)),
        compiler_params=pltpu.CompilerParams(vmem_limit_bytes=VMEM_BYTES),
        cost_estimate=pl.CostEstimate(
            flops=2 * total * width * units,
            bytes_accessed=2 * total * width + 2 * units * width,
            transcendentals=0,
        ),
        name="weight_grads",
    )(*operands)


def pack_kernel(
    step, quarters, routes, probs, tokens, grad_out, *refs
):
    outs, (dense, sem) = refs[:4], refs[4:]
    width = tokens.shape[1]
    copies = []
    for i, out in enumerate(outs):
        place = pl.ds(pl.multiple_of(quarters[i] * step, step), step)
        copies.append(
            pltpu.make_async_copy(tokens.at[place, :], out.at[:, pl.ds(0, width)], sem.at[2 * i])
        )
        copies.append(
            pltpu.make_async_copy(
                grad_out.at[place, :], out.at[:, pl.ds(width, width)], sem.at[2 * i + 1]
            )
        )
    for copy in copies:
        copy.start()
    named = routes[...]
    given = probs[...].astype(F32)
    lanes = dense.shape[1]
    ids = lax.broadcasted_iota(jnp.int32, (lanes, named.shape[1]), 0)
    spread = jnp.zeros(ids.shape, F32)
    for k in range(named.shape[0]):
        spread = spread + jnp.where(ids == named[k : k + 1, :], given[k : k + 1, :], 0.0)
    dense[...] = spread.T
    for copy in copies:
        copy.wait()
    for i, out in enumerate(outs):
        place = pl.ds(pl.multiple_of(quarters[i] * step, step), step)
        out[:, 2 * width :] = dense[place, :].astype(BF16)


def pack(quarters, routes, probs, tokens, grad_out, lanes):
    rows, width = tokens.shape
    step = rows // 4
    return pl.pallas_call(
        functools.partial(pack_kernel, step),
        out_shape=(jax.ShapeDtypeStruct((step, 2 * width + lanes), BF16),) * 4,
        in_specs=[pl.BlockSpec(memory_space=pltpu.SMEM)]
        + [pl.BlockSpec(memory_space=pltpu.VMEM)] * 2
        + [pl.BlockSpec(memory_space=pltpu.HBM)] * 2,
        out_specs=(pl.BlockSpec(memory_space=pltpu.VMEM),) * 4,
        scratch_shapes=[pltpu.VMEM((rows, lanes), F32), pltpu.SemaphoreType.DMA((8,))],
        name="pack",
    )(quarters, routes.T, probs.T, tokens, grad_out)


def after(value, *others):
    return lax.optimization_barrier((value, *others))[0] if others else value


def gathered_body(tokens, grad_out, routes, probs, w_gate, w_up, w_down):
    lines = 4
    axes = ("expert", "etp")
    local_experts, hid_units, width = w_gate.shape
    expert_count = 2 * lines * local_experts
    units = local_experts * hid_units
    tok_rows, top_count = routes.shape
    step = tok_rows // 4
    expert, etp = lax.axis_index("expert"), lax.axis_index("etp")
    side, core = etp // 2, etp % 2

    order = (0, 2, 3, 1)
    places = [
        (z, y, x, c) for z in range(lines) for y in range(2) for x in range(2) for c in range(2)
    ]

    def number(z, y, x, c):
        return ((z * 2 + y) * 2 + x) * 2 + c

    def along(hops):
        ahead = {order[i]: order[(i + hops) % lines] for i in range(lines)}
        return [(number(z, y, x, c), number(ahead[z], y, x, c)) for z, y, x, c in places]

    over_y = [(number(z, y, x, c), number(z, 1 - y, x, c)) for z, y, x, c in places]
    over_x = [(number(z, y, x, c), number(z, y, 1 - x, c)) for z, y, x, c in places]
    over_c = [(number(z, y, x, c), number(z, y, x, 1 - c)) for z, y, x, c in places]

    def move(value, pairs):
        return lax.ppermute(value, axes, pairs)

    extra = -(-expert_count // LANES) * LANES
    ids = jnp.arange(extra, dtype=jnp.int32)

    quarters = jnp.stack(
        [2 * x + c for x, c in ((side, core), (1 - side, core), (side, 1 - core), (1 - side, 1 - core))]
    ).astype(jnp.int32)
    here, near, *rest = pack(quarters, routes, probs, tokens, grad_out, extra)
    gate_up = jnp.concatenate([w_gate.reshape(units, width), w_up.reshape(units, width)], axis=0)
    down = w_down.reshape(units, width)
    base = (expert * local_experts).astype(jnp.int32).reshape(1)

    line = {0: here, 1: move(here, along(1))}
    line[2] = move(line[1], along(1))
    line[3] = move(after(here, line[2]), along(-1))
    other = {s: move(line[s], over_y) for s in range(lines)}
    line_x = {0: near, 1: move(line[1], over_x), 3: move(after(near, line[3]), along(-1))}
    other_x = {0: move(near, over_y)}
    ready, line_x[1], gate_up = lax.optimization_barrier((other[1], line_x[1], gate_up))
    first = move(jnp.concatenate([ready, line[2]], axis=0), over_x)
    rows, grads, chips, fars, backs = {}, {}, {}, {}, {}
    sequence = list(range(lines))
    for s in sequence:
        if s == 0:
            other_x[0] = after(other_x[0], line[2])
        mine = jnp.concatenate([line[s], line_x[s], other[s], other_x[s]], axis=0)
        if s == 0:
            theirs = jnp.concatenate(rest + [move(mine[2 * step :], over_c)], axis=0)
        else:
            theirs = move(mine, over_c)
        wait = [chips[s - 1]] if s > 1 else []
        keep, send, d_both, hid = stage(after(base, *wait), mine, theirs, gate_up, down, local_experts)
        rows[s], grads[s] = (mine, theirs), (d_both, hid)
        chips[s] = keep.astype(F32) + move(send, over_c).astype(F32)
        fars[s] = move(chips[s][2 * step :].astype(BF16), over_y)
        if s == 0:
            _, pair, other[2], other[3], line_x[3] = lax.optimization_barrier(
                (hid, first, other[2], other[3], line_x[3])
            )
            other_x[1], line_x[2] = pair[:step], pair[step:]
            second = move(jnp.concatenate([other[2], other[3]], axis=0), over_x)
        elif s == 1:
            _, pair, fars[0] = lax.optimization_barrier((hid, second, fars[0]))
            other_x[2], other_x[3] = pair[:step], pair[step:]
        elif s == 2:
            _, fars[1] = lax.optimization_barrier((hid, fars[1]))
            backs[1] = move((chips[1][: 2 * step] + fars[1].astype(F32)).astype(BF16), along(-1))
        elif s == 3:
            _, fars[2] = lax.optimization_barrier((hid, fars[2]))
    hids = [rows[s] + (grads[s][1],) for s in sequence]
    boths = [rows[s] + (grads[s][0],) for s in sequence]
    held = chips[2][: 2 * step] + fars[2].astype(F32)
    passed = move(held.astype(BF16), along(1))
    hids[-1] = hids[-1][:2] + (after(hids[-1][2], held, chips[3]),)
    grad_down = weight_grads(hids, 1, width, units)
    grad_down, fars[3], passed, backs[1] = lax.optimization_barrier(
        (grad_down, fars[3], passed, backs[1])
    )
    held = chips[3][: 2 * step] + fars[3].astype(F32) + passed.astype(F32)
    backs[3] = move(held.astype(BF16), along(1))
    boths[-1] = boths[-1][:2] + (after(boths[-1][2], grad_down, held),)
    grad_gate = weight_grads(boths, 0, width, units)
    grad_gate, backs[3] = lax.optimization_barrier((grad_gate, backs[3]))
    total = chips[0][: 2 * step] + fars[0].astype(F32)
    for back in backs.values():
        total = total + back.astype(F32)
    total = total.astype(BF16)
    cross = move(total, over_x)
    boths[-1] = boths[-1][:2] + (after(boths[-1][2], total),)
    grad_up = weight_grads(boths, 0, width, units, 1)
    grad_up, cross = lax.optimization_barrier((grad_up, cross))
    final = (
        total.astype(F32) + jnp.concatenate([cross[step:], cross[:step]], axis=0).astype(F32)
    ).astype(BF16)
    beside = move(final, over_c)

    pair = jnp.stack([final, beside]).reshape(2, 2, step, -1)
    pair = jnp.where(core == 0, pair, pair[::-1])
    pair = jnp.where(side == 0, pair, pair[:, ::-1])
    whole = jnp.transpose(pair, (1, 0, 2, 3)).reshape(tok_rows, -1)
    grad_tokens = whole[:, :width]
    found = whole[:, None, width:]
    named = routes[:, :, None] == ids
    grad_probs = jnp.sum(jnp.where(named, found, 0).astype(F32), axis=2).astype(BF16)
    shape = w_gate.shape
    return (
        grad_tokens,
        grad_probs,
        grad_gate.reshape(shape),
        grad_up.reshape(shape),
        grad_down.reshape(shape),
    )


def body(sources, splits, tokens, grad_out, routes, probs, w_gate, w_up, w_down):
    tok_rows, top_count = routes.shape
    local_experts = w_gate.shape[0]
    slots = local_experts * slots_of(tok_rows, top_count, sources * local_experts)
    fits = splits == 4 and sources == 8 and tok_rows % 64 == 0
    args = (tokens, grad_out, routes, probs, w_gate, w_up, w_down)
    if fits and slots >= tok_rows:
        return gathered_body(*args)
    return routed_body(*args)


def solution(mesh):
    return jax.shard_map(
        functools.partial(body, mesh.shape["expert"], mesh.shape["etp"]),
        mesh=mesh,
        in_specs=(
            P("expert", None),
            P("expert", None),
            P("expert", None),
            P("expert", None),
            P("expert", "etp", None),
            P("expert", "etp", None),
            P("expert", "etp", None),
        ),
        out_specs=(
            P("expert", None),
            P("expert", None),
            P("expert", "etp", None),
            P("expert", "etp", None),
            P("expert", "etp", None),
        ),
        check_vma=False,
    )
```

```python
import functools

import jax
import jax.numpy as jnp
from jax import lax
from jax.experimental import pallas as pl
from jax.experimental.pallas import tpu as pltpu
from jax.sharding import PartitionSpec as P

BF16 = jnp.bfloat16
F32 = jnp.float32
LANES = 128
VMEM_BYTES = 16 * 1024 * 1024


def token_sum(slot_rows, target, tok_rows, top_count):
    columns = slot_rows.shape[-1]
    picked = slot_rows.reshape(-1, columns)[target]
    return jnp.sum(picked.reshape(tok_rows, top_count, columns).astype(F32), axis=1).astype(BF16)


def expert_major(values, sources, local_experts, capacity):
    tail = values.shape[2:]
    shaped = values.reshape((sources, local_experts, capacity) + tail)
    order = (1, 0, 2) + tuple(range(3, 3 + len(tail)))
    return jnp.transpose(shaped, order).reshape((local_experts, sources * capacity) + tail)


def source_major(values, sources, local_experts, capacity):
    tail = values.shape[2:]
    shaped = values.reshape((local_experts, sources, capacity) + tail)
    order = (1, 0, 2) + tuple(range(3, 3 + len(tail)))
    return jnp.transpose(shaped, order).reshape((sources, local_experts * capacity) + tail)


def slots_of(tok_rows, top_count, expert_count):
    return max(2, 5 * tok_rows * top_count // (4 * expert_count))


def routed_body(tokens, grad_out, routes, probs, w_gate, w_up, w_down):
    sources = lax.axis_size("expert")
    local_experts = w_gate.shape[0]
    hid_units = w_gate.shape[1]
    expert_count = sources * local_experts
    tok_rows, top_count = routes.shape
    model_width = tokens.shape[1]
    capacity = slots_of(tok_rows, top_count, expert_count)
    pair_count = tok_rows * top_count
    flat_routes = routes.reshape(-1)
    one_hot = (flat_routes[:, None] == jnp.arange(expert_count, dtype=jnp.int32)[None, :]).astype(
        jnp.int32
    )
    slot_rank = jnp.sum(jnp.cumsum(one_hot, axis=0) * one_hot, axis=1) - 1
    target = flat_routes * capacity + slot_rank
    slot_table = (
        jnp.full((expert_count * capacity,), pair_count, jnp.int32)
        .at[target]
        .set(jnp.arange(pair_count, dtype=jnp.int32))
    )
    filled = slot_table < pair_count
    safe_index = jnp.where(filled, slot_table, 0)
    token_of = safe_index // top_count
    block_rows = local_experts * capacity
    send_prob = jnp.where(filled, probs.reshape(-1)[safe_index], 0).reshape(sources, block_rows)
    send_rows = jnp.where(filled[:, None], tokens[token_of], 0).reshape(
        sources, block_rows, model_width
    )
    send_grad = jnp.where(filled[:, None], grad_out[token_of], 0).reshape(
        sources, block_rows, model_width
    )
    recv_rows, recv_grad, recv_prob = (
        lax.all_to_all(send_rows, "expert", split_axis=0, concat_axis=0, tiled=True),
        lax.all_to_all(send_grad, "expert", split_axis=0, concat_axis=0, tiled=True),
        lax.all_to_all(send_prob, "expert", split_axis=0, concat_axis=0, tiled=True),
    )
    in_rows = expert_major(recv_rows, sources, local_experts, capacity)
    in_grad = expert_major(recv_grad, sources, local_experts, capacity)
    weight = expert_major(recv_prob, sources, local_experts, capacity).astype(F32)[..., None]
    gate_up = jnp.concatenate([w_gate, w_up], axis=1)
    both_pre = jnp.einsum("end,ehd->enh", in_rows, gate_up, preferred_element_type=F32)
    pre_gate = both_pre[..., :hid_units]
    pre_up = both_pre[..., hid_units:]
    back_grad = jnp.einsum("end,ehd->enh", in_grad, w_down, preferred_element_type=F32)
    sigma_gate = jax.nn.sigmoid(pre_gate)
    activated = pre_gate * sigma_gate
    hidden = (activated * pre_up).astype(BF16)
    prob_local = jnp.sum(hidden.astype(F32) * back_grad, axis=-1)
    prob_part = source_major(prob_local, sources, local_experts, capacity)
    scaled = (weight * in_grad.astype(F32)).astype(BF16)
    grad_down = jnp.einsum("enh,end->ehd", hidden, scaled, preferred_element_type=F32).astype(BF16)
    hidden_grad = weight * back_grad
    d_gate = (hidden_grad * pre_up * sigma_gate * (1.0 + pre_gate * (1.0 - sigma_gate))).astype(
        BF16
    )
    d_up = (hidden_grad * activated).astype(BF16)
    d_both = jnp.concatenate([d_gate, d_up], axis=-1)
    grad_both = jnp.einsum("enh,end->ehd", d_both, in_rows, preferred_element_type=F32).astype(BF16)
    grad_gate = grad_both[:, :hid_units]
    grad_up = grad_both[:, hid_units:]
    local_part = jnp.einsum("enh,ehd->end", d_both, gate_up, preferred_element_type=F32).astype(
        BF16
    )
    partial_sum = source_major(local_part, sources, local_experts, capacity).astype(F32)
    totals, prob_total = (
        lax.psum(partial_sum.astype(BF16), "etp").astype(F32),
        lax.psum(prob_part.astype(BF16), "etp").astype(F32),
    )
    back_rows, back_prob = (
        lax.all_to_all(totals.astype(BF16), "expert", split_axis=0, concat_axis=0, tiled=True),
        lax.all_to_all(prob_total.astype(BF16), "expert", split_axis=0, concat_axis=0, tiled=True),
    )
    grad_tokens = token_sum(back_rows, target, tok_rows, top_count)
    grad_probs = back_prob.reshape(-1)[target].reshape(tok_rows, top_count)
    return (grad_tokens, grad_probs, grad_gate, grad_up, grad_down)


def stage_kernel(local_experts, base_ref, mine, theirs, gate_up, down, keep, send, d_both, hid):
    units, width = down.shape
    each = units // local_experts
    half = mine.shape[0]
    count = 2 * half
    nt = (((1,), (1,)), ((), ()))

    def both(start, stop):
        return jnp.concatenate([mine[:, start:stop], theirs[:, start:stop]], axis=0)

    pre = lax.dot_general(both(0, width), gate_up[...], nt, preferred_element_type=F32)
    back = lax.dot_general(both(width, 2 * width), down[...], nt, preferred_element_type=F32)
    extra = both(2 * width, mine.shape[1]).astype(F32)
    lane = lax.broadcasted_iota(jnp.int32, extra.shape, 1)
    unit = lax.broadcasted_iota(jnp.int32, (count, units), 1)
    weight = jnp.zeros((count, units), F32)
    for e in range(local_experts):
        own = jnp.sum(jnp.where(lane == base_ref[0] + e, extra, 0.0), axis=1, keepdims=True)
        weight = jnp.where((unit >= e * each) & (unit < (e + 1) * each), own, weight)
    pre_gate = pre[:, :units]
    pre_up = pre[:, units:]
    sigma = 1.0 / (1.0 + jnp.exp(-pre_gate))
    activated = pre_gate * sigma
    hidden = (activated * pre_up).astype(BF16).astype(F32)
    product = hidden * back
    found = jnp.zeros(extra.shape, F32)
    for e in range(local_experts):
        covered = (unit >= e * each) & (unit < (e + 1) * each)
        own = jnp.sum(jnp.where(covered, product, 0.0), axis=1, keepdims=True)
        found = jnp.where(lane == base_ref[0] + e, own, found)
    hid[...] = (hidden * weight).astype(BF16)
    hidden_grad = weight * back
    d_both[:, :units] = (
        hidden_grad * pre_up * sigma * (1.0 + pre_gate * (1.0 - sigma))
    ).astype(BF16)
    d_both[:, units:] = (hidden_grad * activated).astype(BF16)
    part = jnp.dot(d_both[...], gate_up[...], preferred_element_type=F32).astype(BF16)
    keep[:, :width] = part[:half]
    send[:, :width] = part[half:]
    keep[:, width:] = found[:half].astype(BF16)
    send[:, width:] = found[half:].astype(BF16)


def stage(base, mine, theirs, gate_up, down, local_experts):
    units, width = down.shape
    half, columns = mine.shape
    count = 2 * half
    extra = columns - 2 * width
    flops = 2 * count * width * (2 * units + units + 2 * units)
    return pl.pallas_call(
        functools.partial(stage_kernel, local_experts),
        out_shape=(
            jax.ShapeDtypeStruct((half, width + extra), BF16),
            jax.ShapeDtypeStruct((half, width + extra), BF16),
            jax.ShapeDtypeStruct((count, 2 * units), BF16),
            jax.ShapeDtypeStruct((count, units), BF16),
        ),
        in_specs=[pl.BlockSpec(memory_space=pltpu.SMEM)]
        + [pl.BlockSpec(memory_space=pltpu.VMEM)] * 4,
        out_specs=(pl.BlockSpec(memory_space=pltpu.VMEM),) * 4,
        compiler_params=pltpu.CompilerParams(vmem_limit_bytes=VMEM_BYTES),
        cost_estimate=pl.CostEstimate(
            flops=flops, bytes_accessed=4 * count * columns, transcendentals=count * units
        ),
        name="stage",
    )(base, mine, theirs, gate_up, down)


def weights_kernel(stages, *refs):
    out = refs[-1]
    tn = (((0,), (0,)), ((), ()))
    total = 0.0
    for s in range(stages):
        mine, theirs, hid = refs[3 * s : 3 * s + 3]
        rows = jnp.concatenate([mine[...], theirs[...]], axis=0)
        total = total + lax.dot_general(hid[...], rows, tn, preferred_element_type=F32)
    out[...] = total.astype(BF16)


def weight_grads(parts, side, width, units, which=0):
    tile = 512
    tiles = width // tile
    specs, operands, total = [], [], 0
    for mine, theirs, hid in parts:
        half = mine.shape[0]
        total += 2 * half
        specs += [pl.BlockSpec((half, tile), lambda j: (0, j + side * tiles))] * 2
        specs += [pl.BlockSpec((2 * half, units), lambda j: (0, which))]
        operands += [pltpu.with_memory_space_constraint(v, pltpu.HBM) for v in (mine, theirs, hid)]
    return pl.pallas_call(
        functools.partial(weights_kernel, len(parts)),
        grid=(tiles,),
        out_shape=jax.ShapeDtypeStruct((units, width), BF16),
        in_specs=specs,
        out_specs=pl.BlockSpec((units, tile), lambda j: (0, j)),
        compiler_params=pltpu.CompilerParams(vmem_limit_bytes=VMEM_BYTES),
        cost_estimate=pl.CostEstimate(
            flops=2 * total * width * units,
            bytes_accessed=2 * total * width + 2 * units * width,
            transcendentals=0,
        ),
        name="weight_grads",
    )(*operands)


def quarter_of(etp, i):
    side, core = etp // 2, etp % 2
    x = 1 - side if i % 2 else side
    c = 1 - core if i // 2 else core
    return 2 * x + c


def pack_kernel(step, first, etp, routes, probs, tokens, grad_out, *refs):
    outs, (dense, sem) = refs[:-2], refs[-2:]
    width = tokens.shape[1]
    places = [
        pl.ds(pl.multiple_of(quarter_of(etp[0], first + i) * step, step), step)
        for i in range(len(outs))
    ]
    copies = []
    for i, (out, place) in enumerate(zip(outs, places)):
        for j, rows in enumerate((tokens, grad_out)):
            copies.append(
                pltpu.make_async_copy(
                    rows.at[place, :], out.at[:, pl.ds(j * width, width)], sem.at[2 * i + j]
                )
            )
    for copy in copies:
        copy.start()
    named = routes[...]
    given = probs[...].astype(F32)
    lanes = dense.shape[1]
    ids = lax.broadcasted_iota(jnp.int32, (lanes, named.shape[1]), 0)
    spread = jnp.zeros(ids.shape, F32)
    for k in range(named.shape[0]):
        spread = spread + jnp.where(ids == named[k : k + 1, :], given[k : k + 1, :], 0.0)
    dense[...] = spread.T
    for out, place in zip(outs, places):
        out[:, 2 * width :] = dense[place, :].astype(BF16)
    for copy in copies:
        copy.wait()


def pack(first, count, etp, routes, probs, tokens, grad_out, lanes):
    rows, width = tokens.shape
    step = rows // 4
    return pl.pallas_call(
        functools.partial(pack_kernel, step, first),
        out_shape=(jax.ShapeDtypeStruct((step, 2 * width + lanes), BF16),) * count,
        in_specs=[pl.BlockSpec(memory_space=pltpu.SMEM)]
        + [pl.BlockSpec(memory_space=pltpu.VMEM)] * 2
        + [pl.BlockSpec(memory_space=pltpu.HBM)] * 2,
        out_specs=(pl.BlockSpec(memory_space=pltpu.VMEM),) * count,
        scratch_shapes=[
            pltpu.VMEM((rows, lanes), F32),
            pltpu.SemaphoreType.DMA((2 * count,)),
        ],
        name="pack",
    )(etp, routes.T, probs.T, tokens, grad_out)


def unpack_kernel(etp, routes, near, far, rows, weights, found):
    width = rows.shape[1]
    step = near.shape[0] // 2
    for i in range(4):
        place = pl.ds(pl.multiple_of(quarter_of(etp[0], i) * step, step), step)
        part = (near, far)[i // 2][(i % 2) * step : (i % 2 + 1) * step, :]
        rows[place, :] = part[:, :width]
        found[place, :] = part[:, width:].astype(F32)
    flipped = found[...].T
    named = routes[...]
    ids = lax.broadcasted_iota(jnp.int32, flipped.shape, 0)
    for k in range(named.shape[0]):
        own = jnp.where(ids == named[k : k + 1, :], flipped, 0.0)
        weights[k : k + 1, :] = jnp.sum(own, axis=0, keepdims=True).astype(BF16)


def unpack(etp, routes, near, far, width):
    rows, top_count = routes.shape
    out, picked = pl.pallas_call(
        unpack_kernel,
        out_shape=(
            jax.ShapeDtypeStruct((rows, width), BF16),
            jax.ShapeDtypeStruct((top_count, rows), BF16),
        ),
        in_specs=[pl.BlockSpec(memory_space=pltpu.SMEM)]
        + [pl.BlockSpec(memory_space=pltpu.VMEM)] * 3,
        out_specs=(pl.BlockSpec(memory_space=pltpu.VMEM),) * 2,
        scratch_shapes=[pltpu.VMEM((rows, near.shape[1] - width), F32)],
        name="unpack",
    )(etp, routes.T, near, far)
    return out, picked.T


def after(value, *others):
    return lax.optimization_barrier((value, *others))[0] if others else value


def gathered_body(tokens, grad_out, routes, probs, w_gate, w_up, w_down):
    lines = 4
    axes = ("expert", "etp")
    local_experts, hid_units, width = w_gate.shape
    expert_count = 2 * lines * local_experts
    units = local_experts * hid_units
    tok_rows, top_count = routes.shape
    step = tok_rows // 4
    expert, etp = lax.axis_index("expert"), lax.axis_index("etp")

    order = (0, 2, 3, 1)
    places = [
        (z, y, x, c) for z in range(lines) for y in range(2) for x in range(2) for c in range(2)
    ]

    def number(z, y, x, c):
        return ((z * 2 + y) * 2 + x) * 2 + c

    def along(hops):
        ahead = {order[i]: order[(i + hops) % lines] for i in range(lines)}
        return [(number(z, y, x, c), number(ahead[z], y, x, c)) for z, y, x, c in places]

    over_y = [(number(z, y, x, c), number(z, 1 - y, x, c)) for z, y, x, c in places]
    over_x = [(number(z, y, x, c), number(z, y, 1 - x, c)) for z, y, x, c in places]
    over_c = [(number(z, y, x, c), number(z, y, x, 1 - c)) for z, y, x, c in places]

    def move(value, pairs):
        return lax.ppermute(value, axes, pairs)

    extra = -(-expert_count // LANES) * LANES
    place = etp.astype(jnp.int32).reshape(1)
    (here,) = pack(0, 1, place, routes, probs, tokens, grad_out, extra)
    near, *rest = pack(1, 3, place, routes, probs, tokens, grad_out, extra)
    gate_up = jnp.concatenate([w_gate.reshape(units, width), w_up.reshape(units, width)], axis=0)
    down = w_down.reshape(units, width)
    base = (expert * local_experts).astype(jnp.int32).reshape(1)

    line = {0: here, 1: move(here, along(1))}
    line[2] = move(line[1], along(1))
    line[3] = move(after(here, line[2]), along(-1))
    other = {s: move(line[s], over_y) for s in range(lines)}
    line_x = {0: near, 1: move(line[1], over_x), 3: move(after(near, line[3]), along(-1))}
    other_x = {0: move(near, over_y)}
    ready, line_x[1], gate_up = lax.optimization_barrier((other[1], line_x[1], gate_up))
    other_x[1] = move(ready, over_x)
    pair = move(jnp.concatenate([line[2], after(other[2], line[3])], axis=0), over_x)
    rows, grads, chips, fars, backs = {}, {}, {}, {}, {}
    sequence = list(range(lines))
    for s in sequence:
        if s == 0:
            other_x[0] = after(other_x[0], line[2])
        mine = jnp.concatenate([line[s], line_x[s], other[s], other_x[s]], axis=0)
        if s == 0:
            theirs = jnp.concatenate(rest + [move(mine[2 * step :], over_c)], axis=0)
        else:
            theirs = move(mine, over_c)
        wait = [chips[s - 1]] if s > 1 else []
        if s == 3:
            wait += [fars[1]]
        keep, send, d_both, hid = stage(after(base, *wait), mine, theirs, gate_up, down, local_experts)
        rows[s], grads[s] = (mine, theirs), (d_both, hid)
        chips[s] = keep.astype(F32) + move(send, over_c).astype(F32)
        if s:
            fars[s] = move(chips[s][2 * step :].astype(BF16), over_y)
        if s == 0:
            _, other_x[1], other[3], line_x[3] = lax.optimization_barrier(
                (hid, other_x[1], other[3], line_x[3])
            )
            other_x[3] = move(other[3], over_x)
        elif s == 1:
            _, pair = lax.optimization_barrier((hid, pair))
            line_x[2], other_x[2] = pair[:step], pair[step:]
        elif s == 2:
            _, other_x[3] = lax.optimization_barrier((hid, other_x[3]))
            backs[1] = move((chips[1][: 2 * step] + fars[1].astype(F32)).astype(BF16), along(-1))
        elif s == 3:
            _, fars[2] = lax.optimization_barrier((hid, fars[2]))
    hids = [rows[s] + (grads[s][1],) for s in sequence]
    boths = [rows[s] + (grads[s][0],) for s in sequence]
    held = chips[2][: 2 * step] + fars[2].astype(F32)
    passed = move(held.astype(BF16), along(1))
    hids[-1] = hids[-1][:2] + (after(hids[-1][2], held, chips[3]),)
    grad_down = weight_grads(hids, 1, width, units)
    grad_down, fars[3], passed, backs[1] = lax.optimization_barrier(
        (grad_down, fars[3], passed, backs[1])
    )
    held = chips[3][: 2 * step] + fars[3].astype(F32) + passed.astype(F32)
    backs[3] = move(held.astype(BF16), along(1))
    fars[0] = move(after(chips[0][2 * step :].astype(BF16), held), over_y)
    boths[-1] = boths[-1][:2] + (after(boths[-1][2], grad_down, held),)
    grad_gate = weight_grads(boths, 0, width, units)
    grad_gate, backs[3], fars[0] = lax.optimization_barrier((grad_gate, backs[3], fars[0]))
    total = chips[0][: 2 * step] + fars[0].astype(F32)
    for back in backs.values():
        total = total + back.astype(F32)
    total = total.astype(BF16)
    cross = move(total, over_x)
    boths[-1] = boths[-1][:2] + (after(boths[-1][2], total),)
    grad_up = weight_grads(boths, 0, width, units, 1)
    grad_up, cross = lax.optimization_barrier((grad_up, cross))
    final = (
        total.astype(F32) + jnp.concatenate([cross[step:], cross[:step]], axis=0).astype(F32)
    ).astype(BF16)
    beside = move(final, over_c)

    grad_tokens, grad_probs = unpack(place, routes, final, beside, width)
    shape = w_gate.shape
    return (
        grad_tokens,
        grad_probs,
        grad_gate.reshape(shape),
        grad_up.reshape(shape),
        grad_down.reshape(shape),
    )


def body(sources, splits, tokens, grad_out, routes, probs, w_gate, w_up, w_down):
    tok_rows, top_count = routes.shape
    local_experts = w_gate.shape[0]
    slots = local_experts * slots_of(tok_rows, top_count, sources * local_experts)
    fits = splits == 4 and sources == 8 and tok_rows % 64 == 0
    args = (tokens, grad_out, routes, probs, w_gate, w_up, w_down)
    if fits and slots >= tok_rows:
        return gathered_body(*args)
    return routed_body(*args)


def solution(mesh):
    return jax.shard_map(
        functools.partial(body, mesh.shape["expert"], mesh.shape["etp"]),
        mesh=mesh,
        in_specs=(
            P("expert", None),
            P("expert", None),
            P("expert", None),
            P("expert", None),
            P("expert", "etp", None),
            P("expert", "etp", None),
            P("expert", "etp", None),
        ),
        out_specs=(
            P("expert", None),
            P("expert", None),
            P("expert", "etp", None),
            P("expert", "etp", None),
            P("expert", "etp", None),
        ),
        check_vma=False,
    )
```

```python
import functools

import jax
import jax.numpy as jnp
from jax import lax
from jax.experimental import pallas as pl
from jax.experimental.pallas import tpu as pltpu
from jax.sharding import PartitionSpec as P

BF16 = jnp.bfloat16
F32 = jnp.float32
LANES = 128
VMEM_BYTES = 16 * 1024 * 1024


def token_sum(slot_rows, target, tok_rows, top_count):
    columns = slot_rows.shape[-1]
    picked = slot_rows.reshape(-1, columns)[target]
    return jnp.sum(picked.reshape(tok_rows, top_count, columns).astype(F32), axis=1).astype(BF16)


def expert_major(values, sources, local_experts, capacity):
    tail = values.shape[2:]
    shaped = values.reshape((sources, local_experts, capacity) + tail)
    order = (1, 0, 2) + tuple(range(3, 3 + len(tail)))
    return jnp.transpose(shaped, order).reshape((local_experts, sources * capacity) + tail)


def source_major(values, sources, local_experts, capacity):
    tail = values.shape[2:]
    shaped = values.reshape((local_experts, sources, capacity) + tail)
    order = (1, 0, 2) + tuple(range(3, 3 + len(tail)))
    return jnp.transpose(shaped, order).reshape((sources, local_experts * capacity) + tail)


def slots_of(tok_rows, top_count, expert_count):
    return max(2, 5 * tok_rows * top_count // (4 * expert_count))


def routed_body(tokens, grad_out, routes, probs, w_gate, w_up, w_down):
    sources = lax.axis_size("expert")
    local_experts = w_gate.shape[0]
    hid_units = w_gate.shape[1]
    expert_count = sources * local_experts
    tok_rows, top_count = routes.shape
    model_width = tokens.shape[1]
    capacity = slots_of(tok_rows, top_count, expert_count)
    pair_count = tok_rows * top_count
    flat_routes = routes.reshape(-1)
    one_hot = (flat_routes[:, None] == jnp.arange(expert_count, dtype=jnp.int32)[None, :]).astype(
        jnp.int32
    )
    slot_rank = jnp.sum(jnp.cumsum(one_hot, axis=0) * one_hot, axis=1) - 1
    target = flat_routes * capacity + slot_rank
    slot_table = (
        jnp.full((expert_count * capacity,), pair_count, jnp.int32)
        .at[target]
        .set(jnp.arange(pair_count, dtype=jnp.int32))
    )
    filled = slot_table < pair_count
    safe_index = jnp.where(filled, slot_table, 0)
    token_of = safe_index // top_count
    block_rows = local_experts * capacity
    send_prob = jnp.where(filled, probs.reshape(-1)[safe_index], 0).reshape(sources, block_rows)
    send_rows = jnp.where(filled[:, None], tokens[token_of], 0).reshape(
        sources, block_rows, model_width
    )
    send_grad = jnp.where(filled[:, None], grad_out[token_of], 0).reshape(
        sources, block_rows, model_width
    )
    recv_rows, recv_grad, recv_prob = (
        lax.all_to_all(send_rows, "expert", split_axis=0, concat_axis=0, tiled=True),
        lax.all_to_all(send_grad, "expert", split_axis=0, concat_axis=0, tiled=True),
        lax.all_to_all(send_prob, "expert", split_axis=0, concat_axis=0, tiled=True),
    )
    in_rows = expert_major(recv_rows, sources, local_experts, capacity)
    in_grad = expert_major(recv_grad, sources, local_experts, capacity)
    weight = expert_major(recv_prob, sources, local_experts, capacity).astype(F32)[..., None]
    gate_up = jnp.concatenate([w_gate, w_up], axis=1)
    both_pre = jnp.einsum("end,ehd->enh", in_rows, gate_up, preferred_element_type=F32)
    pre_gate = both_pre[..., :hid_units]
    pre_up = both_pre[..., hid_units:]
    back_grad = jnp.einsum("end,ehd->enh", in_grad, w_down, preferred_element_type=F32)
    sigma_gate = jax.nn.sigmoid(pre_gate)
    activated = pre_gate * sigma_gate
    hidden = (activated * pre_up).astype(BF16)
    prob_local = jnp.sum(hidden.astype(F32) * back_grad, axis=-1)
    prob_part = source_major(prob_local, sources, local_experts, capacity)
    scaled = (weight * in_grad.astype(F32)).astype(BF16)
    grad_down = jnp.einsum("enh,end->ehd", hidden, scaled, preferred_element_type=F32).astype(BF16)
    hidden_grad = weight * back_grad
    d_gate = (hidden_grad * pre_up * sigma_gate * (1.0 + pre_gate * (1.0 - sigma_gate))).astype(
        BF16
    )
    d_up = (hidden_grad * activated).astype(BF16)
    d_both = jnp.concatenate([d_gate, d_up], axis=-1)
    grad_both = jnp.einsum("enh,end->ehd", d_both, in_rows, preferred_element_type=F32).astype(BF16)
    grad_gate = grad_both[:, :hid_units]
    grad_up = grad_both[:, hid_units:]
    local_part = jnp.einsum("enh,ehd->end", d_both, gate_up, preferred_element_type=F32).astype(
        BF16
    )
    partial_sum = source_major(local_part, sources, local_experts, capacity).astype(F32)
    totals, prob_total = (
        lax.psum(partial_sum.astype(BF16), "etp").astype(F32),
        lax.psum(prob_part.astype(BF16), "etp").astype(F32),
    )
    back_rows, back_prob = (
        lax.all_to_all(totals.astype(BF16), "expert", split_axis=0, concat_axis=0, tiled=True),
        lax.all_to_all(prob_total.astype(BF16), "expert", split_axis=0, concat_axis=0, tiled=True),
    )
    grad_tokens = token_sum(back_rows, target, tok_rows, top_count)
    grad_probs = back_prob.reshape(-1)[target].reshape(tok_rows, top_count)
    return (grad_tokens, grad_probs, grad_gate, grad_up, grad_down)


def stage_kernel(local_experts, base_ref, mine, theirs, gate_up, down, keep, send, d_both, hid):
    units, width = down.shape
    each = units // local_experts
    half = mine.shape[0]
    count = 2 * half
    nt = (((1,), (1,)), ((), ()))

    def both(start, stop):
        return jnp.concatenate([mine[:, start:stop], theirs[:, start:stop]], axis=0)

    pre = lax.dot_general(both(0, width), gate_up[...], nt, preferred_element_type=F32)
    back = lax.dot_general(both(width, 2 * width), down[...], nt, preferred_element_type=F32)
    extra = both(2 * width, mine.shape[1]).astype(F32)
    lane = lax.broadcasted_iota(jnp.int32, extra.shape, 1)
    unit = lax.broadcasted_iota(jnp.int32, (count, units), 1)
    weight = jnp.zeros((count, units), F32)
    for e in range(local_experts):
        own = jnp.sum(jnp.where(lane == base_ref[0] + e, extra, 0.0), axis=1, keepdims=True)
        weight = jnp.where((unit >= e * each) & (unit < (e + 1) * each), own, weight)
    pre_gate = pre[:, :units]
    pre_up = pre[:, units:]
    sigma = 1.0 / (1.0 + jnp.exp(-pre_gate))
    activated = pre_gate * sigma
    hidden = (activated * pre_up).astype(BF16).astype(F32)
    product = hidden * back
    found = jnp.zeros(extra.shape, F32)
    for e in range(local_experts):
        covered = (unit >= e * each) & (unit < (e + 1) * each)
        own = jnp.sum(jnp.where(covered, product, 0.0), axis=1, keepdims=True)
        found = jnp.where(lane == base_ref[0] + e, own, found)
    hid[...] = (hidden * weight).astype(BF16)
    hidden_grad = weight * back
    d_both[:, :units] = (
        hidden_grad * pre_up * sigma * (1.0 + pre_gate * (1.0 - sigma))
    ).astype(BF16)
    d_both[:, units:] = (hidden_grad * activated).astype(BF16)
    part = jnp.dot(d_both[...], gate_up[...], preferred_element_type=F32).astype(BF16)
    keep[:, :width] = part[:half]
    send[:, :width] = part[half:]
    keep[:, width:] = found[:half].astype(BF16)
    send[:, width:] = found[half:].astype(BF16)


def stage(base, mine, theirs, gate_up, down, local_experts):
    units, width = down.shape
    half, columns = mine.shape
    count = 2 * half
    extra = columns - 2 * width
    flops = 2 * count * width * (2 * units + units + 2 * units)
    return pl.pallas_call(
        functools.partial(stage_kernel, local_experts),
        out_shape=(
            jax.ShapeDtypeStruct((half, width + extra), BF16),
            jax.ShapeDtypeStruct((half, width + extra), BF16),
            jax.ShapeDtypeStruct((count, 2 * units), BF16),
            jax.ShapeDtypeStruct((count, units), BF16),
        ),
        in_specs=[pl.BlockSpec(memory_space=pltpu.SMEM)]
        + [pl.BlockSpec(memory_space=pltpu.VMEM)] * 4,
        out_specs=(pl.BlockSpec(memory_space=pltpu.VMEM),) * 4,
        compiler_params=pltpu.CompilerParams(vmem_limit_bytes=VMEM_BYTES),
        cost_estimate=pl.CostEstimate(
            flops=flops, bytes_accessed=4 * count * columns, transcendentals=count * units
        ),
        name="stage",
    )(base, mine, theirs, gate_up, down)


def weights_kernel(stages, *refs):
    out = refs[-1]
    tn = (((0,), (0,)), ((), ()))
    total = 0.0
    for s in range(stages):
        mine, theirs, hid = refs[3 * s : 3 * s + 3]
        rows = jnp.concatenate([mine[...], theirs[...]], axis=0)
        total = total + lax.dot_general(hid[...], rows, tn, preferred_element_type=F32)
    out[...] = total.astype(BF16)


def weight_grads(parts, side, width, units, which=0):
    tile = 512
    tiles = width // tile
    specs, operands, total = [], [], 0
    for mine, theirs, hid in parts:
        half = mine.shape[0]
        total += 2 * half
        specs += [pl.BlockSpec((half, tile), lambda j: (0, j + side * tiles))] * 2
        specs += [pl.BlockSpec((2 * half, units), lambda j: (0, which))]
        operands += [pltpu.with_memory_space_constraint(v, pltpu.HBM) for v in (mine, theirs, hid)]
    return pl.pallas_call(
        functools.partial(weights_kernel, len(parts)),
        grid=(tiles,),
        out_shape=jax.ShapeDtypeStruct((units, width), BF16),
        in_specs=specs,
        out_specs=pl.BlockSpec((units, tile), lambda j: (0, j)),
        compiler_params=pltpu.CompilerParams(vmem_limit_bytes=VMEM_BYTES),
        cost_estimate=pl.CostEstimate(
            flops=2 * total * width * units,
            bytes_accessed=2 * total * width + 2 * units * width,
            transcendentals=0,
        ),
        name="weight_grads",
    )(*operands)


def quarter_of(etp, i):
    side, core = etp // 2, etp % 2
    x = 1 - side if i % 2 else side
    c = 1 - core if i // 2 else core
    return 2 * x + c


def pack_kernel(step, first, etp, routes, probs, tokens, grad_out, *refs):
    outs, (dense, sem) = refs[:-2], refs[-2:]
    width = tokens.shape[1]
    places = [
        pl.ds(pl.multiple_of(quarter_of(etp[0], first + i) * step, step), step)
        for i in range(len(outs))
    ]
    copies = []
    for i, (out, place) in enumerate(zip(outs, places)):
        for j, rows in enumerate((tokens, grad_out)):
            copies.append(
                pltpu.make_async_copy(
                    rows.at[place, :], out.at[:, pl.ds(j * width, width)], sem.at[2 * i + j]
                )
            )
    for copy in copies:
        copy.start()
    named = routes[...]
    given = probs[...].astype(F32)
    lanes = dense.shape[1]
    ids = lax.broadcasted_iota(jnp.int32, (lanes, named.shape[1]), 0)
    spread = jnp.zeros(ids.shape, F32)
    for k in range(named.shape[0]):
        spread = spread + jnp.where(ids == named[k : k + 1, :], given[k : k + 1, :], 0.0)
    dense[...] = spread.T
    for out, place in zip(outs, places):
        out[:, 2 * width :] = dense[place, :].astype(BF16)
    for copy in copies:
        copy.wait()


def pack(first, count, etp, routes, probs, tokens, grad_out, lanes):
    rows, width = tokens.shape
    step = rows // 4
    return pl.pallas_call(
        functools.partial(pack_kernel, step, first),
        out_shape=(jax.ShapeDtypeStruct((step, 2 * width + lanes), BF16),) * count,
        in_specs=[pl.BlockSpec(memory_space=pltpu.SMEM)]
        + [pl.BlockSpec(memory_space=pltpu.VMEM)] * 2
        + [pl.BlockSpec(memory_space=pltpu.HBM)] * 2,
        out_specs=(pl.BlockSpec(memory_space=pltpu.VMEM),) * count,
        scratch_shapes=[
            pltpu.VMEM((rows, lanes), F32),
            pltpu.SemaphoreType.DMA((2 * count,)),
        ],
        name="pack",
    )(etp, routes.T, probs.T, tokens, grad_out)


def unpack_kernel(etp, routes, near, far, rows, weights, found):
    width = rows.shape[1]
    step = near.shape[0] // 2
    for i in range(4):
        place = pl.ds(pl.multiple_of(quarter_of(etp[0], i) * step, step), step)
        part = (near, far)[i // 2][(i % 2) * step : (i % 2 + 1) * step, :]
        rows[place, :] = part[:, :width]
        found[place, :] = part[:, width:].astype(F32)
    flipped = found[...].T
    named = routes[...]
    ids = lax.broadcasted_iota(jnp.int32, flipped.shape, 0)
    for k in range(named.shape[0]):
        own = jnp.where(ids == named[k : k + 1, :], flipped, 0.0)
        weights[k : k + 1, :] = jnp.sum(own, axis=0, keepdims=True).astype(BF16)


def unpack(etp, routes, near, far, width):
    rows, top_count = routes.shape
    out, picked = pl.pallas_call(
        unpack_kernel,
        out_shape=(
            jax.ShapeDtypeStruct((rows, width), BF16),
            jax.ShapeDtypeStruct((top_count, rows), BF16),
        ),
        in_specs=[pl.BlockSpec(memory_space=pltpu.SMEM)]
        + [pl.BlockSpec(memory_space=pltpu.VMEM)] * 3,
        out_specs=(pl.BlockSpec(memory_space=pltpu.VMEM),) * 2,
        scratch_shapes=[pltpu.VMEM((rows, near.shape[1] - width), F32)],
        compiler_params=pltpu.CompilerParams(vmem_limit_bytes=VMEM_BYTES),
        name="unpack",
    )(etp, routes.T, near, far)
    return out, picked.T


def after(value, *others):
    return lax.optimization_barrier((value, *others))[0] if others else value


def gathered_body(tokens, grad_out, routes, probs, w_gate, w_up, w_down):
    lines = 4
    axes = ("expert", "etp")
    local_experts, hid_units, width = w_gate.shape
    expert_count = 2 * lines * local_experts
    units = local_experts * hid_units
    tok_rows, top_count = routes.shape
    step = tok_rows // 4
    expert, etp = lax.axis_index("expert"), lax.axis_index("etp")

    order = (0, 2, 3, 1)
    places = [
        (z, y, x, c) for z in range(lines) for y in range(2) for x in range(2) for c in range(2)
    ]

    def number(z, y, x, c):
        return ((z * 2 + y) * 2 + x) * 2 + c

    def along(hops):
        ahead = {order[i]: order[(i + hops) % lines] for i in range(lines)}
        return [(number(z, y, x, c), number(ahead[z], y, x, c)) for z, y, x, c in places]

    over_y = [(number(z, y, x, c), number(z, 1 - y, x, c)) for z, y, x, c in places]
    over_x = [(number(z, y, x, c), number(z, y, 1 - x, c)) for z, y, x, c in places]
    over_c = [(number(z, y, x, c), number(z, y, x, 1 - c)) for z, y, x, c in places]

    def move(value, pairs):
        return lax.ppermute(value, axes, pairs)

    extra = -(-expert_count // LANES) * LANES
    place = etp.astype(jnp.int32).reshape(1)
    (here,) = pack(0, 1, place, routes, probs, tokens, grad_out, extra)
    near, *rest = pack(1, 3, place, routes, probs, tokens, grad_out, extra)
    gate_up = jnp.concatenate([w_gate.reshape(units, width), w_up.reshape(units, width)], axis=0)
    down = w_down.reshape(units, width)
    base = (expert * local_experts).astype(jnp.int32).reshape(1)

    line = {0: here, 1: move(here, along(1))}
    line[2] = move(line[1], along(1))
    line[3] = move(after(here, line[2]), along(-1))
    other = {s: move(line[s], over_y) for s in range(lines)}
    line_x = {0: near, 1: move(line[1], over_x), 3: move(after(near, line[3]), along(-1))}
    other_x = {0: move(near, over_y)}
    ready, line_x[1], gate_up = lax.optimization_barrier((other[1], line_x[1], gate_up))
    other_x[1] = move(ready, over_x)
    pair = move(jnp.concatenate([line[2], after(other[2], line[3])], axis=0), over_x)
    rows, grads, chips, fars, backs = {}, {}, {}, {}, {}
    sequence = list(range(lines))
    for s in sequence:
        if s == 0:
            other_x[0] = after(other_x[0], line[2])
        mine = jnp.concatenate([line[s], line_x[s], other[s], other_x[s]], axis=0)
        if s == 0:
            theirs = jnp.concatenate(rest + [move(mine[2 * step :], over_c)], axis=0)
        else:
            theirs = move(mine, over_c)
        wait = [chips[s - 1]] if s > 1 else []
        if s == 3:
            wait += [fars[1]]
        keep, send, d_both, hid = stage(after(base, *wait), mine, theirs, gate_up, down, local_experts)
        rows[s], grads[s] = (mine, theirs), (d_both, hid)
        chips[s] = keep.astype(F32) + move(send, over_c).astype(F32)
        if s:
            fars[s] = move(chips[s][2 * step :].astype(BF16), over_y)
        if s == 0:
            _, other_x[1], other[3], line_x[3] = lax.optimization_barrier(
                (hid, other_x[1], other[3], line_x[3])
            )
            other_x[3] = move(other[3], over_x)
        elif s == 1:
            _, pair = lax.optimization_barrier((hid, pair))
            line_x[2], other_x[2] = pair[:step], pair[step:]
        elif s == 2:
            _, other_x[3] = lax.optimization_barrier((hid, other_x[3]))
            backs[1] = move((chips[1][: 2 * step] + fars[1].astype(F32)).astype(BF16), along(-1))
        elif s == 3:
            _, fars[2] = lax.optimization_barrier((hid, fars[2]))
    hids = [rows[s] + (grads[s][1],) for s in sequence]
    boths = [rows[s] + (grads[s][0],) for s in sequence]
    held = chips[2][: 2 * step] + fars[2].astype(F32)
    passed = move(held.astype(BF16), along(1))
    hids[-1] = hids[-1][:2] + (after(hids[-1][2], held, chips[3]),)
    grad_down = weight_grads(hids, 1, width, units)
    grad_down, fars[3], passed, backs[1] = lax.optimization_barrier(
        (grad_down, fars[3], passed, backs[1])
    )
    held = chips[3][: 2 * step] + fars[3].astype(F32) + passed.astype(F32)
    backs[3] = move(held.astype(BF16), along(1))
    fars[0] = move(after(chips[0][2 * step :].astype(BF16), held), over_y)
    boths[-1] = boths[-1][:2] + (after(boths[-1][2], grad_down, held),)
    grad_gate = weight_grads(boths, 0, width, units)
    grad_gate, backs[3], fars[0] = lax.optimization_barrier((grad_gate, backs[3], fars[0]))
    total = chips[0][: 2 * step] + fars[0].astype(F32)
    for back in backs.values():
        total = total + back.astype(F32)
    total = total.astype(BF16)
    cross = move(total, over_x)
    boths[-1] = boths[-1][:2] + (after(boths[-1][2], total),)
    grad_up = weight_grads(boths, 0, width, units, 1)
    grad_up, cross = lax.optimization_barrier((grad_up, cross))
    final = (
        total.astype(F32) + jnp.concatenate([cross[step:], cross[:step]], axis=0).astype(F32)
    ).astype(BF16)
    beside = move(final, over_c)

    grad_tokens, grad_probs = unpack(place, routes, final, beside, width)
    shape = w_gate.shape
    return (
        grad_tokens,
        grad_probs,
        grad_gate.reshape(shape),
        grad_up.reshape(shape),
        grad_down.reshape(shape),
    )


def body(sources, splits, tokens, grad_out, routes, probs, w_gate, w_up, w_down):
    tok_rows, top_count = routes.shape
    local_experts = w_gate.shape[0]
    slots = local_experts * slots_of(tok_rows, top_count, sources * local_experts)
    fits = splits == 4 and sources == 8 and tok_rows % 64 == 0
    args = (tokens, grad_out, routes, probs, w_gate, w_up, w_down)
    if fits and slots >= tok_rows:
        return gathered_body(*args)
    return routed_body(*args)


def solution(mesh):
    return jax.shard_map(
        functools.partial(body, mesh.shape["expert"], mesh.shape["etp"]),
        mesh=mesh,
        in_specs=(
            P("expert", None),
            P("expert", None),
            P("expert", None),
            P("expert", None),
            P("expert", "etp", None),
            P("expert", "etp", None),
            P("expert", "etp", None),
        ),
        out_specs=(
            P("expert", None),
            P("expert", None),
            P("expert", "etp", None),
            P("expert", "etp", None),
            P("expert", "etp", None),
        ),
        check_vma=False,
    )
```

```python
import functools

import jax
import jax.numpy as jnp
from jax import lax
from jax.experimental import pallas as pl
from jax.experimental.pallas import tpu as pltpu
from jax.sharding import PartitionSpec as P

BF16 = jnp.bfloat16
F32 = jnp.float32
LANES = 128
VMEM_BYTES = 16 * 1024 * 1024


def token_sum(slot_rows, target, tok_rows, top_count):
    columns = slot_rows.shape[-1]
    picked = slot_rows.reshape(-1, columns)[target]
    return jnp.sum(picked.reshape(tok_rows, top_count, columns).astype(F32), axis=1).astype(BF16)


def expert_major(values, sources, local_experts, capacity):
    tail = values.shape[2:]
    shaped = values.reshape((sources, local_experts, capacity) + tail)
    order = (1, 0, 2) + tuple(range(3, 3 + len(tail)))
    return jnp.transpose(shaped, order).reshape((local_experts, sources * capacity) + tail)


def source_major(values, sources, local_experts, capacity):
    tail = values.shape[2:]
    shaped = values.reshape((local_experts, sources, capacity) + tail)
    order = (1, 0, 2) + tuple(range(3, 3 + len(tail)))
    return jnp.transpose(shaped, order).reshape((sources, local_experts * capacity) + tail)


def slots_of(tok_rows, top_count, expert_count):
    return max(2, 5 * tok_rows * top_count // (4 * expert_count))


def routed_body(tokens, grad_out, routes, probs, w_gate, w_up, w_down):
    sources = lax.axis_size("expert")
    local_experts = w_gate.shape[0]
    hid_units = w_gate.shape[1]
    expert_count = sources * local_experts
    tok_rows, top_count = routes.shape
    model_width = tokens.shape[1]
    capacity = slots_of(tok_rows, top_count, expert_count)
    pair_count = tok_rows * top_count
    flat_routes = routes.reshape(-1)
    one_hot = (flat_routes[:, None] == jnp.arange(expert_count, dtype=jnp.int32)[None, :]).astype(
        jnp.int32
    )
    slot_rank = jnp.sum(jnp.cumsum(one_hot, axis=0) * one_hot, axis=1) - 1
    target = flat_routes * capacity + slot_rank
    slot_table = (
        jnp.full((expert_count * capacity,), pair_count, jnp.int32)
        .at[target]
        .set(jnp.arange(pair_count, dtype=jnp.int32))
    )
    filled = slot_table < pair_count
    safe_index = jnp.where(filled, slot_table, 0)
    token_of = safe_index // top_count
    block_rows = local_experts * capacity
    send_prob = jnp.where(filled, probs.reshape(-1)[safe_index], 0).reshape(sources, block_rows)
    send_rows = jnp.where(filled[:, None], tokens[token_of], 0).reshape(
        sources, block_rows, model_width
    )
    send_grad = jnp.where(filled[:, None], grad_out[token_of], 0).reshape(
        sources, block_rows, model_width
    )
    recv_rows, recv_grad, recv_prob = (
        lax.all_to_all(send_rows, "expert", split_axis=0, concat_axis=0, tiled=True),
        lax.all_to_all(send_grad, "expert", split_axis=0, concat_axis=0, tiled=True),
        lax.all_to_all(send_prob, "expert", split_axis=0, concat_axis=0, tiled=True),
    )
    in_rows = expert_major(recv_rows, sources, local_experts, capacity)
    in_grad = expert_major(recv_grad, sources, local_experts, capacity)
    weight = expert_major(recv_prob, sources, local_experts, capacity).astype(F32)[..., None]
    gate_up = jnp.concatenate([w_gate, w_up], axis=1)
    both_pre = jnp.einsum("end,ehd->enh", in_rows, gate_up, preferred_element_type=F32)
    pre_gate = both_pre[..., :hid_units]
    pre_up = both_pre[..., hid_units:]
    back_grad = jnp.einsum("end,ehd->enh", in_grad, w_down, preferred_element_type=F32)
    sigma_gate = jax.nn.sigmoid(pre_gate)
    activated = pre_gate * sigma_gate
    hidden = (activated * pre_up).astype(BF16)
    prob_local = jnp.sum(hidden.astype(F32) * back_grad, axis=-1)
    prob_part = source_major(prob_local, sources, local_experts, capacity)
    scaled = (weight * in_grad.astype(F32)).astype(BF16)
    grad_down = jnp.einsum("enh,end->ehd", hidden, scaled, preferred_element_type=F32).astype(BF16)
    hidden_grad = weight * back_grad
    d_gate = (hidden_grad * pre_up * sigma_gate * (1.0 + pre_gate * (1.0 - sigma_gate))).astype(
        BF16
    )
    d_up = (hidden_grad * activated).astype(BF16)
    d_both = jnp.concatenate([d_gate, d_up], axis=-1)
    grad_both = jnp.einsum("enh,end->ehd", d_both, in_rows, preferred_element_type=F32).astype(BF16)
    grad_gate = grad_both[:, :hid_units]
    grad_up = grad_both[:, hid_units:]
    local_part = jnp.einsum("enh,ehd->end", d_both, gate_up, preferred_element_type=F32).astype(
        BF16
    )
    partial_sum = source_major(local_part, sources, local_experts, capacity).astype(F32)
    totals, prob_total = (
        lax.psum(partial_sum.astype(BF16), "etp").astype(F32),
        lax.psum(prob_part.astype(BF16), "etp").astype(F32),
    )
    back_rows, back_prob = (
        lax.all_to_all(totals.astype(BF16), "expert", split_axis=0, concat_axis=0, tiled=True),
        lax.all_to_all(prob_total.astype(BF16), "expert", split_axis=0, concat_axis=0, tiled=True),
    )
    grad_tokens = token_sum(back_rows, target, tok_rows, top_count)
    grad_probs = back_prob.reshape(-1)[target].reshape(tok_rows, top_count)
    return (grad_tokens, grad_probs, grad_gate, grad_up, grad_down)


def stage_kernel(local_experts, base_ref, mine, theirs, gate_up, down, keep, send, d_both, hid):
    units, width = down.shape
    each = units // local_experts
    half = mine.shape[0]
    count = 2 * half
    nt = (((1,), (1,)), ((), ()))

    def both(start, stop):
        return jnp.concatenate([mine[:, start:stop], theirs[:, start:stop]], axis=0)

    pre = lax.dot_general(both(0, width), gate_up[...], nt, preferred_element_type=F32)
    back = lax.dot_general(both(width, 2 * width), down[...], nt, preferred_element_type=F32)
    extra = both(2 * width, mine.shape[1]).astype(F32)
    lane = lax.broadcasted_iota(jnp.int32, extra.shape, 1)
    unit = lax.broadcasted_iota(jnp.int32, (count, units), 1)
    weight = jnp.zeros((count, units), F32)
    for e in range(local_experts):
        own = jnp.sum(jnp.where(lane == base_ref[0] + e, extra, 0.0), axis=1, keepdims=True)
        weight = jnp.where((unit >= e * each) & (unit < (e + 1) * each), own, weight)
    pre_gate = pre[:, :units]
    pre_up = pre[:, units:]
    sigma = 1.0 / (1.0 + jnp.exp(-pre_gate))
    activated = pre_gate * sigma
    hidden = (activated * pre_up).astype(BF16).astype(F32)
    product = hidden * back
    found = jnp.zeros(extra.shape, F32)
    for e in range(local_experts):
        covered = (unit >= e * each) & (unit < (e + 1) * each)
        own = jnp.sum(jnp.where(covered, product, 0.0), axis=1, keepdims=True)
        found = jnp.where(lane == base_ref[0] + e, own, found)
    hid[...] = (hidden * weight).astype(BF16)
    hidden_grad = weight * back
    d_both[:, :units] = (
        hidden_grad * pre_up * sigma * (1.0 + pre_gate * (1.0 - sigma))
    ).astype(BF16)
    d_both[:, units:] = (hidden_grad * activated).astype(BF16)
    part = jnp.dot(d_both[...], gate_up[...], preferred_element_type=F32).astype(BF16)
    keep[:, :width] = part[:half]
    send[:, :width] = part[half:]
    keep[:, width:] = found[:half].astype(BF16)
    send[:, width:] = found[half:].astype(BF16)


def stage(base, mine, theirs, gate_up, down, local_experts):
    units, width = down.shape
    half, columns = mine.shape
    count = 2 * half
    extra = columns - 2 * width
    flops = 2 * count * width * (2 * units + units + 2 * units)
    return pl.pallas_call(
        functools.partial(stage_kernel, local_experts),
        out_shape=(
            jax.ShapeDtypeStruct((half, width + extra), BF16),
            jax.ShapeDtypeStruct((half, width + extra), BF16),
            jax.ShapeDtypeStruct((count, 2 * units), BF16),
            jax.ShapeDtypeStruct((count, units), BF16),
        ),
        in_specs=[pl.BlockSpec(memory_space=pltpu.SMEM)]
        + [pl.BlockSpec(memory_space=pltpu.VMEM)] * 4,
        out_specs=(pl.BlockSpec(memory_space=pltpu.VMEM),) * 4,
        compiler_params=pltpu.CompilerParams(vmem_limit_bytes=VMEM_BYTES),
        cost_estimate=pl.CostEstimate(
            flops=flops, bytes_accessed=4 * count * columns, transcendentals=count * units
        ),
        name="stage",
    )(base, mine, theirs, gate_up, down)


def weights_kernel(stages, *refs):
    out = refs[-1]
    tn = (((0,), (0,)), ((), ()))
    total = 0.0
    for s in range(stages):
        mine, theirs, hid = refs[3 * s : 3 * s + 3]
        rows = jnp.concatenate([mine[...], theirs[...]], axis=0)
        total = total + lax.dot_general(hid[...], rows, tn, preferred_element_type=F32)
    out[...] = total.astype(BF16)


def weight_grads(parts, side, width, units, which=0):
    tile = 512
    tiles = width // tile
    specs, operands, total = [], [], 0
    for mine, theirs, hid in parts:
        half = mine.shape[0]
        total += 2 * half
        specs += [pl.BlockSpec((half, tile), lambda j: (0, j + side * tiles))] * 2
        specs += [pl.BlockSpec((2 * half, units), lambda j: (0, which))]
        operands += [pltpu.with_memory_space_constraint(v, pltpu.HBM) for v in (mine, theirs, hid)]
    return pl.pallas_call(
        functools.partial(weights_kernel, len(parts)),
        grid=(tiles,),
        out_shape=jax.ShapeDtypeStruct((units, width), BF16),
        in_specs=specs,
        out_specs=pl.BlockSpec((units, tile), lambda j: (0, j)),
        compiler_params=pltpu.CompilerParams(vmem_limit_bytes=VMEM_BYTES),
        cost_estimate=pl.CostEstimate(
            flops=2 * total * width * units,
            bytes_accessed=2 * total * width + 2 * units * width,
            transcendentals=0,
        ),
        name="weight_grads",
    )(*operands)


def quarter_of(etp, i):
    side, core = etp // 2, etp % 2
    x = 1 - side if i % 2 else side
    c = 1 - core if i // 2 else core
    return 2 * x + c


def pack_kernel(step, first, etp, routes, probs, tokens, grad_out, *refs):
    outs, (dense, sem) = refs[:-2], refs[-2:]
    width = tokens.shape[1]
    places = [
        pl.ds(pl.multiple_of(quarter_of(etp[0], first + i) * step, step), step)
        for i in range(len(outs))
    ]
    copies = []
    for i, (out, place) in enumerate(zip(outs, places)):
        for j, rows in enumerate((tokens, grad_out)):
            copies.append(
                pltpu.make_async_copy(
                    rows.at[place, :], out.at[:, pl.ds(j * width, width)], sem.at[2 * i + j]
                )
            )
    for copy in copies:
        copy.start()
    named = routes[...]
    given = probs[...].astype(F32)
    lanes = dense.shape[1]
    ids = lax.broadcasted_iota(jnp.int32, (lanes, named.shape[1]), 0)
    spread = jnp.zeros(ids.shape, F32)
    for k in range(named.shape[0]):
        spread = spread + jnp.where(ids == named[k : k + 1, :], given[k : k + 1, :], 0.0)
    dense[...] = spread.T
    for out, place in zip(outs, places):
        out[:, 2 * width :] = dense[place, :].astype(BF16)
    for copy in copies:
        copy.wait()


def pack(first, count, etp, routes, probs, tokens, grad_out, lanes):
    rows, width = tokens.shape
    step = rows // 4
    return pl.pallas_call(
        functools.partial(pack_kernel, step, first),
        out_shape=(jax.ShapeDtypeStruct((step, 2 * width + lanes), BF16),) * count,
        in_specs=[pl.BlockSpec(memory_space=pltpu.SMEM)]
        + [pl.BlockSpec(memory_space=pltpu.VMEM)] * 2
        + [pl.BlockSpec(memory_space=pltpu.HBM)] * 2,
        out_specs=(pl.BlockSpec(memory_space=pltpu.VMEM),) * count,
        scratch_shapes=[
            pltpu.VMEM((rows, lanes), F32),
            pltpu.SemaphoreType.DMA((2 * count,)),
        ],
        name="pack",
    )(etp, routes.T, probs.T, tokens, grad_out)


def unpack_kernel(etp, routes, near, far, rows, weights, found):
    width = rows.shape[1]
    step = near.shape[0] // 2
    for i in range(4):
        place = pl.ds(pl.multiple_of(quarter_of(etp[0], i) * step, step), step)
        part = (near, far)[i // 2][(i % 2) * step : (i % 2 + 1) * step, :]
        rows[place, :] = part[:, :width]
        found[place, :] = part[:, width:].astype(F32)
    flipped = found[...].T
    named = routes[...]
    ids = lax.broadcasted_iota(jnp.int32, flipped.shape, 0)
    for k in range(named.shape[0]):
        own = jnp.where(ids == named[k : k + 1, :], flipped, 0.0)
        weights[k : k + 1, :] = jnp.sum(own, axis=0, keepdims=True).astype(BF16)


def unpack(etp, routes, near, far, width):
    rows, top_count = routes.shape
    out, picked = pl.pallas_call(
        unpack_kernel,
        out_shape=(
            jax.ShapeDtypeStruct((rows, width), BF16),
            jax.ShapeDtypeStruct((top_count, rows), BF16),
        ),
        in_specs=[pl.BlockSpec(memory_space=pltpu.SMEM)]
        + [pl.BlockSpec(memory_space=pltpu.VMEM)] * 3,
        out_specs=(pl.BlockSpec(memory_space=pltpu.VMEM),) * 2,
        scratch_shapes=[pltpu.VMEM((rows, near.shape[1] - width), F32)],
        compiler_params=pltpu.CompilerParams(vmem_limit_bytes=VMEM_BYTES),
        name="unpack",
    )(etp, routes.T, near, far)
    return out, picked.T


def after(value, *others):
    return lax.optimization_barrier((value, *others))[0] if others else value


def gathered_body(tokens, grad_out, routes, probs, w_gate, w_up, w_down):
    lines = 4
    axes = ("expert", "etp")
    local_experts, hid_units, width = w_gate.shape
    expert_count = 2 * lines * local_experts
    units = local_experts * hid_units
    tok_rows, top_count = routes.shape
    step = tok_rows // 4
    expert, etp = lax.axis_index("expert"), lax.axis_index("etp")

    order = (0, 2, 3, 1)
    places = [
        (z, y, x, c) for z in range(lines) for y in range(2) for x in range(2) for c in range(2)
    ]

    def number(z, y, x, c):
        return ((z * 2 + y) * 2 + x) * 2 + c

    def along(hops):
        ahead = {order[i]: order[(i + hops) % lines] for i in range(lines)}
        return [(number(z, y, x, c), number(ahead[z], y, x, c)) for z, y, x, c in places]

    over_y = [(number(z, y, x, c), number(z, 1 - y, x, c)) for z, y, x, c in places]
    over_x = [(number(z, y, x, c), number(z, y, 1 - x, c)) for z, y, x, c in places]
    over_c = [(number(z, y, x, c), number(z, y, x, 1 - c)) for z, y, x, c in places]

    def move(value, pairs):
        return lax.ppermute(value, axes, pairs)

    extra = -(-expert_count // LANES) * LANES
    place = etp.astype(jnp.int32).reshape(1)
    (here,) = pack(0, 1, place, routes, probs, tokens, grad_out, extra)
    near, *rest = pack(1, 3, place, routes, probs, tokens, grad_out, extra)
    gate_up = jnp.concatenate([w_gate.reshape(units, width), w_up.reshape(units, width)], axis=0)
    down = w_down.reshape(units, width)
    base = (expert * local_experts).astype(jnp.int32).reshape(1)

    line = {0: here, 1: move(here, along(1))}
    line[2] = move(line[1], along(1))
    line[3] = move(after(here, line[2]), along(-1))
    other = {s: move(line[s], over_y) for s in range(lines)}
    line_x = {0: near, 1: move(line[1], over_x), 3: move(after(near, line[3]), along(-1))}
    other_x = {0: move(after(near, other[1]), over_y)}
    ready, line_x[1], gate_up = lax.optimization_barrier((other[1], line_x[1], gate_up))
    other_x[1] = move(ready, over_x)
    pair = move(jnp.concatenate([line[2], after(other[2], line[3])], axis=0), over_x)
    rows, grads, chips, fars, backs = {}, {}, {}, {}, {}
    sequence = list(range(lines))
    for s in sequence:
        if s == 0:
            other_x[0] = after(other_x[0], line[2])
        mine = jnp.concatenate([line[s], line_x[s], other[s], other_x[s]], axis=0)
        if s == 0:
            theirs = jnp.concatenate(rest + [move(mine[2 * step :], over_c)], axis=0)
        else:
            theirs = move(mine, over_c)
        wait = [chips[s - 1]] if s > 1 else []
        if s == 3:
            wait += [fars[1]]
        keep, send, d_both, hid = stage(after(base, *wait), mine, theirs, gate_up, down, local_experts)
        rows[s], grads[s] = (mine, theirs), (d_both, hid)
        chips[s] = keep.astype(F32) + move(send, over_c).astype(F32)
        if s:
            fars[s] = move(chips[s][2 * step :].astype(BF16), over_y)
        if s == 0:
            _, other_x[1], other[3], line_x[3] = lax.optimization_barrier(
                (hid, other_x[1], other[3], line_x[3])
            )
            other_x[3] = move(other[3], over_x)
        elif s == 1:
            _, pair = lax.optimization_barrier((hid, pair))
            line_x[2], other_x[2] = pair[:step], pair[step:]
        elif s == 2:
            _, other_x[3] = lax.optimization_barrier((hid, other_x[3]))
            backs[1] = move((chips[1][: 2 * step] + fars[1].astype(F32)).astype(BF16), along(-1))
        elif s == 3:
            _, fars[2] = lax.optimization_barrier((hid, fars[2]))
    hids = [rows[s] + (grads[s][1],) for s in sequence]
    boths = [rows[s] + (grads[s][0],) for s in sequence]
    held = chips[2][: 2 * step] + fars[2].astype(F32)
    passed = move(held.astype(BF16), along(1))
    hids[-1] = hids[-1][:2] + (after(hids[-1][2], held, chips[3]),)
    grad_down = weight_grads(hids, 1, width, units)
    grad_down, fars[3], passed, backs[1] = lax.optimization_barrier(
        (grad_down, fars[3], passed, backs[1])
    )
    held = chips[3][: 2 * step] + fars[3].astype(F32) + passed.astype(F32)
    backs[3] = move(held.astype(BF16), along(1))
    fars[0] = move(after(chips[0][2 * step :].astype(BF16), held), over_y)
    boths[-1] = boths[-1][:2] + (after(boths[-1][2], grad_down, held),)
    grad_gate = weight_grads(boths, 0, width, units)
    grad_gate, backs[3], fars[0] = lax.optimization_barrier((grad_gate, backs[3], fars[0]))
    total = chips[0][: 2 * step] + fars[0].astype(F32)
    for back in backs.values():
        total = total + back.astype(F32)
    total = total.astype(BF16)
    cross = move(total, over_x)
    boths[-1] = boths[-1][:2] + (after(boths[-1][2], total),)
    grad_up = weight_grads(boths, 0, width, units, 1)
    grad_up, cross = lax.optimization_barrier((grad_up, cross))
    final = (
        total.astype(F32) + jnp.concatenate([cross[step:], cross[:step]], axis=0).astype(F32)
    ).astype(BF16)
    beside = move(final, over_c)

    grad_tokens, grad_probs = unpack(place, routes, final, beside, width)
    shape = w_gate.shape
    return (
        grad_tokens,
        grad_probs,
        grad_gate.reshape(shape),
        grad_up.reshape(shape),
        grad_down.reshape(shape),
    )


def body(sources, splits, tokens, grad_out, routes, probs, w_gate, w_up, w_down):
    tok_rows, top_count = routes.shape
    local_experts = w_gate.shape[0]
    slots = local_experts * slots_of(tok_rows, top_count, sources * local_experts)
    fits = splits == 4 and sources == 8 and tok_rows % 64 == 0
    args = (tokens, grad_out, routes, probs, w_gate, w_up, w_down)
    if fits and slots >= tok_rows:
        return gathered_body(*args)
    return routed_body(*args)


def solution(mesh):
    return jax.shard_map(
        functools.partial(body, mesh.shape["expert"], mesh.shape["etp"]),
        mesh=mesh,
        in_specs=(
            P("expert", None),
            P("expert", None),
            P("expert", None),
            P("expert", None),
            P("expert", "etp", None),
            P("expert", "etp", None),
            P("expert", "etp", None),
        ),
        out_specs=(
            P("expert", None),
            P("expert", None),
            P("expert", "etp", None),
            P("expert", "etp", None),
            P("expert", "etp", None),
        ),
        check_vma=False,
    )
```
